256 devices in a mesh: row: 8 (over z), col: 32 (over y, x, core).
Axes of the slice: x: 4, y: 4, z: 8, core: 2. Of those that a mesh axis runs over, the one named last changes fastest.
Arguments:
- diag_factor: float32 [512, 512], P('row', 'col'), as said below
- panel_factor: float32 [16384, 512], P('row', 'col'), may hold values from -0.046875 to 0.046875
- row_factor: float32 [512, 12288], P('row', 'col'), may hold values from -0.25 to 0.25
- trailing_factor: float32 [16384, 12288], P('row', 'col'), may hold values from -0.046875 to 0.046875
- panel_grad: float32 [16384, 512], P('row', 'col'), may hold values from -6 to 6
- diag_grad: float32 [512, 512], P('row', 'col'), may hold values from -6 to 6
- row_grad: float32 [512, 12288], P('row', 'col'), may hold values from -6 to 6
- trailing_grad: float32 [16384, 12288], P('row', 'col'), may hold values from -6 to 6
Outputs:
- panel_adjoint: float32 [16384, 512], P('row', 'col')
- trailing_out: float32 [16384, 12288], P('row', 'col')
- row_out: float32 [512, 12288], P('row', 'col')
- diag_out: float32 [512, 512], P('row', 'col')
The draws below stay inside these ranges and needn't reach their ends.
Inputs may be any that keep to these rules, and one draw needn't show every extreme that they name: diag_factor is zero above its diagonal; its diagonal entries lie between 1 and 2.
All inputs are finite; a program needn't handle non-finite values.
Results may differ from the reference program's by a relative error of at most 0.00011.
Values sent between devices are 32-bit elements; how exact they have to be, the bound alone decides.
No kernel may reach another device: no remote copies, remote signals or barrier semaphores. Data moves between devices by JAX's collectives and lax.ppermute only.
A program may use at most 64 MiB of HBM per device.

```python
import math
import jax
import jax.numpy as jnp
from jax import lax

B = 512
M = 16384
K = 12288


def draw_diag_factor(key, part):
    first = jax.random.fold_in(key, 11)
    second = jax.random.fold_in(key, 23)
    entries = jax.random.normal(first, (B, B), jnp.float32)
    lower = jnp.tril(entries, -1) / math.sqrt(B)
    diagonal = jax.random.uniform(second, (B,), jnp.float32, 1.0, 2.0)
    return lower + jnp.eye(B, dtype=jnp.float32) * diagonal[None, :]


def level_of(key, dims, pieces, least, top_value):
    loudness = 1.0
    for axis_at, parts in pieces:
        heights = jax.random.uniform(jax.random.fold_in(jax.random.fold_in(key, 6), axis_at), (parts,), jnp.float32, least / len(pieces), top_value / len(pieces))
        loudness = loudness * jnp.repeat(jnp.exp(heights), dims[axis_at] // parts).reshape((-1,) + (1,) * (len(dims) - 1 - axis_at))
    return loudness


def noise(rng, shape, width, most, cuts=(), kind=jnp.bfloat16):
    values = jax.random.normal(rng, shape, jnp.float32) * width
    if len(cuts) > 0:
        values = level_of(rng, shape, cuts, -0.22, 0.18) * values
    return jnp.clip(values, min=-most, max=most).astype(kind)


def setup_inputs(seed: int = 0) -> dict:
    seeds = jax.random.split(jax.random.key(seed), 9)
    return {
        "diag_factor": draw_diag_factor(jax.random.fold_in(seeds[8], 71), 0),
        "panel_factor": noise(seeds[1], (M, B), M ** -0.5, 0.046875, ((0, 8), (1, 32)), jnp.float32),
        "row_factor": noise(seeds[2], (B, K), B ** -0.5, 0.25, ((0, 8), (1, 32)), jnp.float32),
        "trailing_factor": noise(seeds[3], (M, K), M ** -0.5, 0.046875, ((0, 8), (1, 32)), jnp.float32),
        "panel_grad": noise(seeds[4], (M, B), 1.0, 6.0, ((0, 8), (1, 32)), jnp.float32),
        "diag_grad": noise(seeds[5], (B, B), 1.0, 6.0, ((0, 8), (1, 32)), jnp.float32),
        "row_grad": noise(seeds[6], (B, K), 1.0, 6.0, ((0, 8), (1, 32)), jnp.float32),
        "trailing_grad": noise(seeds[7], (M, K), 1.0, 6.0, ((0, 8), (1, 32)), jnp.float32),
    }


def reference(diag_factor, panel_factor, row_factor, trailing_factor, panel_grad, diag_grad, row_grad, trailing_grad):
    high = lax.Precision.HIGHEST
    solved = jax.scipy.linalg.solve_triangular(diag_factor, panel_grad.T, lower=True, trans=1).T
    trailing_out = trailing_grad - jnp.dot(solved.astype(jnp.float32), row_factor.astype(jnp.float32), precision=high, preferred_element_type=jnp.float32)
    row_out = row_grad - jnp.dot(solved.T.astype(jnp.float32), trailing_factor.astype(jnp.float32), precision=high, preferred_element_type=jnp.float32)
    block = diag_grad - jnp.dot(solved.T.astype(jnp.float32), panel_factor.astype(jnp.float32), precision=high, preferred_element_type=jnp.float32)
    diag_out = jnp.tril(block)
    return (solved, trailing_out, row_out, diag_out)
```

```python
import jax
import jax.numpy as jnp
from jax import lax
from jax.experimental import pallas as pl
from jax.experimental.pallas import tpu as pltpu
from jax.sharding import PartitionSpec as P

F32 = jnp.float32
BF16 = jnp.bfloat16
ROWS = 8
COLS = 32
B = 512
MIB = 1 << 20


def with_row_partner(v, k):
    return lax.ppermute(v, "row", [(i, i ^ k) for i in range(ROWS)])


def with_sibling(v):
    return lax.ppermute(v, "col", [(i, i ^ 1) for i in range(COLS)])


def with_col_partner(v, phase, k):
    shift = {0: 1, 1: 3}
    perm = [(i, i ^ (k << shift[phase ^ (i & 1)])) for i in range(COLS)]
    return lax.ppermute(v, "col", perm)


def gather_cols(chunk, core):
    half = chunk.shape[1] // 2
    low, high = chunk[:, :half], chunk[:, half:]
    kept = jnp.where(core == 0, low, high)
    given = jnp.where(core == 0, high, low)
    pair = jnp.concatenate([kept, with_sibling(given)], axis=0)
    quad = jnp.concatenate([pair] + [with_col_partner(pair, 0, k) for k in (1, 2, 3)], axis=0)
    blocks = [quad] + [with_col_partner(quad, 1, k) for k in (2, 1, 3)]
    blocks = [blocks[0], blocks[2], blocks[1], blocks[3]]
    return blocks, [with_sibling(b) for b in blocks]


def place(ids, mine, theirs, store):
    y, x, core = ids[1], ids[2], ids[3]
    for other, blocks in ((0, mine), (1, theirs)):
        half = core ^ other
        for k, block in enumerate(blocks):
            for j in range(4):
                along_x = jnp.where(half == 0, x ^ j, x ^ k)
                along_y = jnp.where(half == 0, y ^ k, y ^ j)
                for r in range(2):
                    row = (along_y * 8 + along_x * 2 + (half ^ r)) * 16
                    at = (j * 2 + r) * 16
                    store(half, pl.multiple_of(row, 16), block[at : at + 16, :])


def split(v):
    high = v.astype(BF16)
    return high, (v - high.astype(F32)).astype(BF16)


def dot3(a, b, contract=((1,), (0,))):
    dims = (contract, ((), ()))
    (ah, al), (bh, bl) = a, b

    def one(p, q):
        return lax.dot_general(p, q, dims, preferred_element_type=F32)

    return one(ah, bh) + (one(ah, bl) + one(al, bh))


def dot_full(a, b):
    return lax.dot_general(
        a, b, (((1,), (0,)), ((), ())), precision=lax.Precision.HIGHEST, preferred_element_type=F32
    )


def invert_kernel(ids, *refs):
    mine, theirs = refs[:4], refs[4:8]
    high_out, low_out, held = refs[8:]

    odd = jnp.broadcast_to(ids[0] % 2, (16, 128)) == 1

    def store(half, row, piece):
        for q in range(2):
            lanes = piece[:, 128 * q : 128 * q + 128]
            swapped = jnp.concatenate([lanes[:, 64:], lanes[:, :64]], axis=1)
            held[(half * 2 + q) ^ (ids[0] // 2), pl.ds(row, 16), :] = jnp.where(odd, swapped, lanes)

    place(ids, mine, theirs, store)

    def part(r, c, n):
        return jnp.concatenate([held[c // 128 + q, r : r + n, :] for q in range(n // 128)], axis=1)

    n = 128
    rows = lax.broadcasted_iota(jnp.int32, (n, n), 0)
    cols = lax.broadcasted_iota(jnp.int32, (n, n), 1)
    in_block = rows // 16 == cols // 16
    diag = [part(n * g, n * g, n) for g in range(4)]
    packed = []
    for d in diag:
        kept = jnp.where(in_block, d, 0.0)
        packed.append(sum(kept[16 * b : 16 * b + 16, :] for b in range(1, 8)) + kept[0:16, :])
    packed = jnp.concatenate(packed, axis=0)
    sub = lax.broadcasted_iota(jnp.int32, (64, n), 0) % 16
    lane = lax.broadcasted_iota(jnp.int32, (64, n), 1) % 16
    inverse = jnp.where(sub == lane, 1.0, 0.0).astype(F32)
    spread = []
    for k in range(16):
        pick = jnp.where(in_block & (rows % 16 == k), 1.0, 0.0).astype(F32)
        spread.append(dot_full(packed, pick))
    for k in range(15, -1, -1):
        factor = spread[k]
        pivot = []
        for g in range(4):
            at = 16 * g + k
            row = inverse[at : at + 1, :] / factor[at : at + 1, :]
            pivot.append(jnp.broadcast_to(row, (16, n)))
        pivot = jnp.concatenate(pivot, axis=0)
        inverse = jnp.where(sub == k, pivot, inverse - jnp.where(sub < k, factor, 0.0) * pivot)
    blocks = []
    for g in range(4):
        tall = jnp.concatenate([inverse[16 * g : 16 * g + 16, :]] * 8, axis=0)
        blocks.append(jnp.where(in_block, tall, 0.0))
    for b in (16, 32, 64):
        off = (rows // (2 * b) == cols // (2 * b)) & (rows // b < cols // b)
        lefts = [dot_full(blocks[g], jnp.where(off, diag[g], 0.0)) for g in range(4)]
        blocks = [blocks[g] - dot_full(lefts[g], blocks[g]) for g in range(4)]
    pairs = []
    for g in (0, 2):
        corner = -dot_full(dot_full(blocks[g], part(n * g, n * g + n, n)), blocks[g + 1])
        top = jnp.concatenate([blocks[g], corner], axis=1)
        low = jnp.concatenate([jnp.zeros_like(corner), blocks[g + 1]], axis=1)
        pairs.append(jnp.concatenate([top, low], axis=0))
    corner = -dot_full(dot_full(pairs[0], part(0, 256, 256)), pairs[1])
    zero = jnp.zeros((256, 256), BF16)
    for out, which in ((high_out, 0), (low_out, 1)):
        out[0:256, 0:256] = split(pairs[0])[which]
        out[0:256, 256:512] = split(corner)[which]
        out[256:512, 0:256] = zero
        out[256:512, 256:512] = split(pairs[1])[which]


def solve_kernel(ids, *refs):
    mine, theirs = refs[:4], refs[4:8]
    inv_high, inv_low, trailing, panel = refs[8:12]
    solved_out, own_out = refs[12:14]
    sends = refs[14:22]
    g_high, g_low, total, corner = refs[22:]

    def store(half, row, piece):
        high, low = split(piece)
        g_high[half, pl.ds(row, 16), :] = high
        g_low[half, pl.ds(row, 16), :] = low

    place(ids, mine, theirs, store)
    total[...] = jnp.zeros_like(total)
    corner[...] = jnp.zeros_like(corner)
    tile = 256
    for half in range(2):

        @pl.loop(0, 1024 // tile)
        def _(step):
            here = pl.ds(pl.multiple_of(step * tile, tile), tile)
            there = pl.ds(pl.multiple_of(half * 1024 + step * tile, tile), tile)
            g = (g_high[half, :, here], g_low[half, :, here])
            g_end = (g[0][256:, :], g[1][256:, :])
            top = dot3((inv_high[0:256, :], inv_low[0:256, :]), g)
            low = dot3((inv_high[256:512, 256:512], inv_low[256:512, 256:512]), g_end)
            x = jnp.concatenate([top, low], axis=0)
            solved_out[:, there] = x
            xs = split(x)
            total[0:512, :] += dot3(xs, split(trailing[there, :]))
            corner[...] += dot3(split(panel[:, there]), xs, ((1,), (1,)))

    own = pl.ds(pl.multiple_of(ids[4] * 16, 16), 16)
    own_out[...] = solved_out[own, :]
    summed = corner[...]
    zero = jnp.zeros((8, 384), F32)
    for t in range(ROWS):
        part = summed[:, 64 * t : 64 * t + 64]
        total[512 + 8 * t : 520 + 8 * t, :] = zero
        total[512 + 8 * t : 520 + 8 * t, 0:64] = part[0:8, :]
        total[512 + 8 * t : 520 + 8 * t, 64:128] = part[8:16, :]
    for k in range(ROWS):
        target = ids[0] ^ k
        sends[k][0:64, :] = total[pl.ds(pl.multiple_of(target * 64, 64), 64), :]
        sends[k][64:72, :] = total[pl.ds(pl.multiple_of(512 + target * 8, 8), 8), :]


def trailing_kernel(ids, *refs):
    pieces = refs[:8]
    solved, grad, out, r_high, r_low = refs[8:]

    @pl.when(pl.program_id(0) == 0)
    def _():
        for k in range(ROWS):
            at = pl.ds(pl.multiple_of((ids[0] ^ k) * 64, 64), 64)
            r_high[at, :], r_low[at, :] = split(pieces[k][...])

    x = split(solved[...].T)
    out[...] = grad[...] - dot3(x, (r_high[...], r_low[...]))


SMEM = pl.BlockSpec(memory_space=pltpu.SMEM)
VMEM = pl.BlockSpec(memory_space=pltpu.VMEM)


def shape(dims, dtype=F32):
    return jax.ShapeDtypeStruct(dims, dtype)


def invert(ids, mine, theirs):
    return pl.pallas_call(
        invert_kernel,
        out_shape=[shape((B, B), BF16)] * 2,
        in_specs=[SMEM] + [VMEM] * 8,
        out_specs=[VMEM] * 2,
        scratch_shapes=[pltpu.VMEM((4, B, 128), F32)],
        compiler_params=pltpu.CompilerParams(vmem_limit_bytes=16 * MIB),
        cost_estimate=pl.CostEstimate(flops=4_000_000_000, bytes_accessed=2 * MIB, transcendentals=0),
        name="invert",
    )(ids, *mine, *theirs)


def solve(ids, mine, theirs, inverse, trailing, panel):
    return pl.pallas_call(
        solve_kernel,
        out_shape=[shape((B, 2048)), shape((16, 2048))] + [shape((72, 384))] * 8,
        in_specs=[SMEM] + [VMEM] * 12,
        out_specs=[VMEM] * 10,
        scratch_shapes=[
            pltpu.VMEM((2, B, 1024), BF16),
            pltpu.VMEM((2, B, 1024), BF16),
            pltpu.VMEM((B + 64, 384), F32),
            pltpu.VMEM((16, B), F32),
        ],
        compiler_params=pltpu.CompilerParams(vmem_limit_bytes=40 * MIB),
        cost_estimate=pl.CostEstimate(flops=5_000_000_000, bytes_accessed=12 * MIB, transcendentals=0),
        name="solve",
    )(ids, *mine, *theirs, *inverse, trailing, panel)


def trailing_update(ids, pieces, solved, grad):
    tile = 256
    return pl.pallas_call(
        trailing_kernel,
        grid=(2048 // tile,),
        out_shape=shape((2048, 384)),
        in_specs=[SMEM]
        + [pl.BlockSpec((64, 384), lambda i: (0, 0))] * 8
        + [pl.BlockSpec((B, tile), lambda i: (0, i)), pl.BlockSpec((tile, 384), lambda i: (i, 0))],
        out_specs=pl.BlockSpec((tile, 384), lambda i: (i, 0)),
        scratch_shapes=[pltpu.VMEM((B, 384), BF16), pltpu.VMEM((B, 384), BF16)],
        compiler_params=pltpu.CompilerParams(vmem_limit_bytes=16 * MIB),
        cost_estimate=pl.CostEstimate(flops=4_000_000_000, bytes_accessed=11 * MIB, transcendentals=0),
        name="trailing",
    )(ids, *pieces, solved, grad)


def on_device(
    diag_factor,
    panel_factor,
    row_factor,
    trailing_factor,
    panel_grad,
    diag_grad,
    row_grad,
    trailing_grad,
):
    z = lax.axis_index("row")
    col = lax.axis_index("col")
    core = col % 2
    ids = jnp.stack([z, col // 8, (col // 2) % 4, core, col]).astype(jnp.int32)

    tile = diag_factor.T
    tiles = [tile] + [with_row_partner(tile, k) for k in range(1, ROWS)]
    diag_chunk = jnp.concatenate(tiles, axis=1)

    diag_mine, diag_theirs = gather_cols(diag_chunk, core)
    grad_mine, grad_theirs = gather_cols(panel_grad.T, core)
    row_pieces = [row_factor] + [with_row_partner(row_factor, k) for k in range(1, ROWS)]

    inverse = invert(ids, diag_mine, diag_theirs)
    solved, own, *sends = solve(ids, grad_mine, grad_theirs, inverse, trailing_factor, panel_factor.T)
    came = [with_row_partner(sends[k], k) for k in range(1, ROWS)]
    trailing_out = trailing_update(ids, row_pieces, solved, trailing_grad)

    total = sends[0]
    for term in came:
        total = total + term
    row_out = row_grad - total[0:64, :]
    diag_sum = jnp.concatenate([total[64:72, 0:64], total[64:72, 64:128]], axis=0)
    global_rows = z * 64 + jnp.arange(64)[None, :]
    global_cols = col * 16 + jnp.arange(16)[:, None]
    diag_out = jnp.where(global_rows >= global_cols, diag_grad.T - diag_sum, jnp.float32(0.0))
    return (own.T, trailing_out, row_out, diag_out.T)


def solution(mesh):
    both = P("row", "col")
    return jax.shard_map(
        on_device,
        mesh=mesh,
        in_specs=(both,) * 8,
        out_specs=(both,) * 4,
        check_vma=False,
    )
```

```python
import jax
import jax.numpy as jnp
from jax import lax
from jax.experimental import pallas as pl
from jax.experimental.pallas import tpu as pltpu
from jax.sharding import PartitionSpec as P

F32 = jnp.float32
BF16 = jnp.bfloat16
ROWS = 8
COLS = 32
B = 512
MIB = 1 << 20


def with_row_partner(v, k):
    return lax.ppermute(v, "row", [(i, i ^ k) for i in range(ROWS)])


def with_sibling(v):
    return lax.ppermute(v, "col", [(i, i ^ 1) for i in range(COLS)])


def with_neighbour(v):
    perm = []
    for r in range(ROWS):
        for c in range(COLS):
            to = r ^ 1 if c % 2 == 0 else (r - 1 + 2 * (r % 2)) % ROWS
            perm.append((r * COLS + c, to * COLS + c))
    return lax.ppermute(v, ("row", "col"), perm)


def with_col_partner(v, phase, k):
    shift = {0: 1, 1: 3}
    perm = [(i, i ^ (k << shift[phase ^ (i & 1)])) for i in range(COLS)]
    return lax.ppermute(v, "col", perm)


def gather_cols(diag, grad, core):
    wide, narrow = grad.shape[1] // 2, diag.shape[1] // 2
    low = jnp.concatenate([grad[:, :wide], diag[:, :narrow]], axis=1)
    high = jnp.concatenate([grad[:, wide:], diag[:, narrow:]], axis=1)
    kept = jnp.where(core == 0, low, high)
    given = jnp.where(core == 0, high, low)
    pair = jnp.concatenate([kept, with_sibling(given)], axis=0)
    pairs = [pair] + [with_col_partner(pair, 0, k) for k in (1, 2, 3)]
    diag_quad = jnp.concatenate([p[:, wide:] for p in pairs], axis=0)
    grad_quad = jnp.concatenate([p[:, :wide] for p in pairs], axis=0)
    diag_blocks = [diag_quad] + [with_col_partner(diag_quad, 1, k) for k in (1, 2, 3)]
    grad_quad, diag_blocks = lax.optimization_barrier((grad_quad, diag_blocks))
    diag_blocks = diag_blocks + [with_sibling(b) for b in diag_blocks]
    return diag_blocks, grad_quad, [with_col_partner(grad_quad, 1, k) for k in (1, 2, 3)]


def place(ids, blocks, store):
    y, x, core = ids[1], ids[2], ids[3]
    for other in range(2):
        half = core ^ other
        for k, block in enumerate(blocks[4 * other : 4 * other + 4]):
            for j in range(4):
                along_x = jnp.where(half == 0, x ^ j, x ^ k)
                along_y = jnp.where(half == 0, y ^ k, y ^ j)
                for r in range(2):
                    row = (along_y * 8 + along_x * 2 + (half ^ r)) * 16
                    at = (j * 2 + r) * 16
                    store(half, pl.multiple_of(row, 16), block[at : at + 16, :])


def split(v):
    high = v.astype(BF16)
    return high, (v - high.astype(F32)).astype(BF16)


def dot(a, b):
    return lax.dot_general(a, b, (((1,), (0,)), ((), ())), preferred_element_type=F32)


def dot_full(a, b):
    return lax.dot_general(
        a, b, (((1,), (0,)), ((), ())), precision=lax.Precision.HIGHEST, preferred_element_type=F32
    )


def invert_kernel(ids, *refs):
    blocks = refs[:8]
    top_out, low_out, held = refs[8:]

    odd = jnp.broadcast_to(ids[0] % 2, (16, 128)) == 1

    def store(half, row, piece):
        for q in range(2):
            lanes = piece[:, 128 * q : 128 * q + 128]
            swapped = jnp.concatenate([lanes[:, 64:], lanes[:, :64]], axis=1)
            held[(half * 2 + q) ^ (ids[0] // 2), pl.ds(row, 16), :] = jnp.where(odd, swapped, lanes)

    place(ids, blocks, store)

    def part(r, c, n):
        return jnp.concatenate([held[c // 128 + q, r : r + n, :] for q in range(n // 128)], axis=1)

    n = 128
    rows = lax.broadcasted_iota(jnp.int32, (n, n), 0)
    cols = lax.broadcasted_iota(jnp.int32, (n, n), 1)
    in_block = rows // 16 == cols // 16
    diag = [part(n * g, n * g, n) for g in range(4)]
    packed = []
    for d in diag:
        kept = jnp.where(in_block, d, 0.0)
        packed.append(sum(kept[16 * b : 16 * b + 16, :] for b in range(1, 8)) + kept[0:16, :])
    packed = jnp.concatenate(packed, axis=0)
    sub = lax.broadcasted_iota(jnp.int32, (64, n), 0) % 16
    lane = lax.broadcasted_iota(jnp.int32, (64, n), 1) % 16
    inverse = jnp.where(sub == lane, 1.0, 0.0).astype(F32)
    spread = []
    for k in range(16):
        pick = jnp.where(in_block & (rows % 16 == k), 1.0, 0.0).astype(F32)
        spread.append(dot_full(packed, pick))
    for k in range(15, -1, -1):
        factor = spread[k]
        pivot = []
        for g in range(4):
            at = 16 * g + k
            row = inverse[at : at + 1, :] / factor[at : at + 1, :]
            pivot.append(jnp.broadcast_to(row, (16, n)))
        pivot = jnp.concatenate(pivot, axis=0)
        inverse = jnp.where(sub == k, pivot, inverse - jnp.where(sub < k, factor, 0.0) * pivot)
    blocks = []
    for g in range(4):
        tall = jnp.concatenate([inverse[16 * g : 16 * g + 16, :]] * 8, axis=0)
        blocks.append(jnp.where(in_block, tall, 0.0))
    for b in (16, 32, 64):
        off = (rows // (2 * b) == cols // (2 * b)) & (rows // b < cols // b)
        lefts = [dot_full(blocks[g], jnp.where(off, diag[g], 0.0)) for g in range(4)]
        blocks = [blocks[g] - dot_full(lefts[g], blocks[g]) for g in range(4)]
    pairs = []
    for g in (0, 2):
        corner = -dot_full(dot_full(blocks[g], part(n * g, n * g + n, n)), blocks[g + 1])
        top = jnp.concatenate([blocks[g], corner], axis=1)
        low = jnp.concatenate([jnp.zeros_like(corner), blocks[g + 1]], axis=1)
        pairs.append(jnp.concatenate([top, low], axis=0))
    corner = -dot_full(dot_full(pairs[0], part(0, 256, 256)), pairs[1])
    for at, out, m in ((0, top_out, pairs[0]), (768, top_out, corner), (0, low_out, pairs[1])):
        high, low = split(m)
        out[:, at : at + 256] = high
        out[:, at + 256 : at + 512] = high
        out[:, at + 512 : at + 768] = low


def split_kernel(trailing, panel, out):
    n = trailing.shape[0]
    side = jnp.concatenate([panel[...], jnp.zeros((112, n), F32)], axis=0).T
    for v, lanes in ((trailing[...], slice(0, 384)), (side, slice(384, 512))):
        high, low = split(v)
        out[0:n, lanes] = high
        out[n : 2 * n, lanes] = low
        out[2 * n : 3 * n, lanes] = high


def solve_kernel(ids, *refs):
    blocks = refs[:8]
    inv_top, inv_low, tall = refs[8:11]
    solved_out, own_out, given_out = refs[11:14]
    kept_outs = refs[14:18]
    g, xs, total, corner = refs[18:]

    def store(half, row, piece):
        high, low = split(piece)
        row = pl.multiple_of(jnp.where(row < 256, row, row + 512), 16)
        g[half, pl.ds(row, 16), :] = high
        g[half, pl.ds(row + 256, 16), :] = low
        g[half, pl.ds(row + 512, 16), :] = high

    place(ids, blocks, store)
    n = TILE
    for t in range(2048 // n):
        half, lane = divmod(t * n, 1024)
        slot = t % 2
        rhs = g[half, :, lane : lane + n]
        for rows, lhs, k in ((slice(0, 256), inv_top, 0), (slice(256, 512), inv_low, 768)):
            x = dot(lhs[...], g[half, k:, lane : lane + n])
            solved_out[rows, t * n : t * n + n] = x
            high, low = split(x)
            xs[slot, rows, 0:n] = high
            xs[slot, rows, n : 2 * n] = high
            xs[slot, rows, 2 * n : 3 * n] = low
        term = dot(xs[slot], tall[3 * n * t : 3 * n * t + 3 * n, :])
        if t == 0:
            total[...] = term
        else:
            total[...] += term

    own = pl.ds(pl.multiple_of(ids[4] * 16, 16), 16)
    own_out[...] = solved_out[own, :]
    corner[...] = jnp.zeros_like(corner)
    summed = total[:, 384:512].T
    for t in range(ROWS):
        corner[t, :, 0:64] = summed[0:8, 64 * t : 64 * t + 64]
        corner[t, :, 64:128] = summed[8:16, 64 * t : 64 * t + 64]
    for j in range(4):
        for first, out, at in ((ids[5], given_out, 72 * j), (ids[0], kept_outs[j], 0)):
            target = first ^ (2 * j)
            out[at : at + 64, :] = total[pl.ds(pl.multiple_of(target * 64, 64), 64), 0:384]
            out[at + 64 : at + 72, :] = corner[target]


def trailing_kernel(ids, *refs):
    own_parity, other_parity = refs[:4], refs[4]
    solved, grad, out, rs = refs[5:]

    @pl.when(pl.program_id(0) == 0)
    def _():
        for j in range(4):
            for first, piece in ((ids[0], own_parity[j][...]), (ids[5], other_parity[64 * j : 64 * j + 64, :])):
                high, low = split(piece)
                row = (first ^ (2 * j)) * 64
                rs[pl.ds(pl.multiple_of(row, 64), 64), :] = high
                rs[pl.ds(pl.multiple_of(row + 512, 64), 64), :] = low
                rs[pl.ds(pl.multiple_of(row + 1024, 64), 64), :] = high

    high, low = split(solved[...].T)
    out[...] = grad[...] - dot(jnp.concatenate([high, high, low], axis=1), rs[...])


TILE = 512
SMEM = pl.BlockSpec(memory_space=pltpu.SMEM)
VMEM = pl.BlockSpec(memory_space=pltpu.VMEM)


def shape(dims, dtype=F32):
    return jax.ShapeDtypeStruct(dims, dtype)


def invert(ids, blocks):
    return pl.pallas_call(
        invert_kernel,
        out_shape=[shape((256, 1536), BF16), shape((256, 768), BF16)],
        in_specs=[SMEM] + [VMEM] * 8,
        out_specs=[VMEM] * 2,
        scratch_shapes=[pltpu.VMEM((4, B, 128), F32)],
        compiler_params=pltpu.CompilerParams(vmem_limit_bytes=10 * MIB),
        cost_estimate=pl.CostEstimate(flops=4_000_000_000, bytes_accessed=2 * MIB, transcendentals=0),
        name="invert",
    )(ids, *blocks)


def split_tall(trailing, panel):
    n = TILE
    return pl.pallas_call(
        split_kernel,
        grid=(2048 // n,),
        out_shape=shape((3 * 2048, 512), BF16),
        in_specs=[pl.BlockSpec((n, 384), lambda i: (i, 0)), pl.BlockSpec((16, n), lambda i: (0, i))],
        out_specs=pl.BlockSpec((3 * n, 512), lambda i: (i, 0)),
        compiler_params=pltpu.CompilerParams(vmem_limit_bytes=10 * MIB),
        cost_estimate=pl.CostEstimate(flops=3_000_000_000, bytes_accessed=9 * MIB, transcendentals=0),
        name="split_tall",
    )(trailing, panel)


def solve(ids, blocks, inverse, tall):
    return pl.pallas_call(
        solve_kernel,
        out_shape=[shape((B, 2048)), shape((16, 2048)), shape((288, 384))] + [shape((72, 384))] * 4,
        in_specs=[SMEM] + [VMEM] * 11,
        out_specs=[VMEM] * 7,
        scratch_shapes=[
            pltpu.VMEM((2, 3 * B, 1024), BF16),
            pltpu.VMEM((2, B, 3 * TILE), BF16),
            pltpu.VMEM((B, 512), F32),
            pltpu.VMEM((ROWS, 8, 384), F32),
        ],
        compiler_params=pltpu.CompilerParams(vmem_limit_bytes=24 * MIB),
        cost_estimate=pl.CostEstimate(flops=6_000_000_000, bytes_accessed=12 * MIB, transcendentals=0),
        name="solve",
    )(ids, *blocks, *inverse, tall)


def trailing_update(ids, pieces, solved, grad):
    tile = 256
    return pl.pallas_call(
        trailing_kernel,
        grid=(2048 // tile,),
        out_shape=shape((2048, 384)),
        in_specs=[SMEM]
        + [pl.BlockSpec((64, 384), lambda i: (0, 0))] * 4
        + [pl.BlockSpec((256, 384), lambda i: (0, 0))]
        + [pl.BlockSpec((B, tile), lambda i: (0, i)), pl.BlockSpec((tile, 384), lambda i: (i, 0))],
        out_specs=pl.BlockSpec((tile, 384), lambda i: (i, 0)),
        scratch_shapes=[pltpu.VMEM((3 * B, 384), BF16)],
        compiler_params=pltpu.CompilerParams(vmem_limit_bytes=10 * MIB),
        cost_estimate=pl.CostEstimate(flops=4_000_000_000, bytes_accessed=11 * MIB, transcendentals=0),
        name="trailing",
    )(ids, *pieces, solved, grad)


def on_device(
    diag_factor,
    panel_factor,
    row_factor,
    trailing_factor,
    panel_grad,
    diag_grad,
    row_grad,
    trailing_grad,
):
    z = lax.axis_index("row")
    col = lax.axis_index("col")
    core = col % 2
    neighbour = jnp.where(core == 0, z ^ 1, (z - 1 + 2 * (z % 2)) % ROWS)
    ids = jnp.stack([z, col // 8, (col // 2) % 4, core, col, neighbour]).astype(jnp.int32)

    tile = diag_factor.T
    even = [tile] + [with_row_partner(tile, k) for k in (2, 4, 6)]
    odd = with_row_partner(jnp.concatenate(even, axis=1), 1)
    tiles = [t for j in range(4) for t in (even[j], odd[:, 64 * j : 64 * j + 64])]
    diag_chunk = jnp.concatenate(tiles, axis=1)
    diag_blocks, grad_quad, grad_far = gather_cols(diag_chunk, panel_grad.T, core)
    quad_swapped = with_sibling(grad_quad)

    row_factor, diag_blocks = lax.optimization_barrier((row_factor, diag_blocks))
    row_pieces = [row_factor] + [with_row_partner(row_factor, k) for k in (2, 4, 6)]
    inverse = invert(ids, diag_blocks)
    tall = split_tall(trailing_factor, panel_factor.T)
    grad_far, row_pieces, inverse, tall = lax.optimization_barrier((grad_far, row_pieces, inverse, tall))
    row_pieces = row_pieces + [with_neighbour(jnp.concatenate(row_pieces, axis=0))]
    grad_blocks = [grad_quad] + grad_far + [quad_swapped] + [with_sibling(b) for b in grad_far]
    solved, own, given, *kept = solve(ids, grad_blocks, inverse, tall)
    taken = with_neighbour(given)
    sums = [kept[j] + taken[72 * j : 72 * j + 72] for j in range(4)]
    came = [with_row_partner(sums[j], 2 * j) for j in range(1, 4)]
    trailing_out = trailing_update(ids, row_pieces, solved, trailing_grad)

    total = sums[0] + (came[0] + came[1] + came[2])
    row_out = row_grad - total[0:64, :]
    diag_sum = jnp.concatenate([total[64:72, 0:64], total[64:72, 64:128]], axis=0)
    global_rows = z * 64 + jnp.arange(64)[None, :]
    global_cols = col * 16 + jnp.arange(16)[:, None]
    diag_out = jnp.where(global_rows >= global_cols, diag_grad.T - diag_sum, jnp.float32(0.0))
    return (own.T, trailing_out, row_out, diag_out.T)


def solution(mesh):
    both = P("row", "col")
    return jax.shard_map(
        on_device,
        mesh=mesh,
        in_specs=(both,) * 8,
        out_specs=(both,) * 4,
        check_vma=False,
    )
```

```python
import jax
import jax.numpy as jnp
from jax import lax
from jax.experimental import pallas as pl
from jax.experimental.pallas import tpu as pltpu
from jax.sharding import PartitionSpec as P

F32 = jnp.float32
BF16 = jnp.bfloat16
ROWS = 8
COLS = 32
B = 512
MIB = 1 << 20


def with_row_partner(v, k):
    return lax.ppermute(v, "row", [(i, i ^ k) for i in range(ROWS)])


def with_sibling(v):
    return lax.ppermute(v, "col", [(i, i ^ 1) for i in range(COLS)])


def with_neighbour(v):
    perm = []
    for r in range(ROWS):
        for c in range(COLS):
            to = r ^ 1 if c % 2 == 0 else (r - 1 + 2 * (r % 2)) % ROWS
            perm.append((r * COLS + c, to * COLS + c))
    return lax.ppermute(v, ("row", "col"), perm)


def with_col_partner(v, phase, k):
    shift = {0: 1, 1: 3}
    perm = [(i, i ^ (k << shift[phase ^ (i & 1)])) for i in range(COLS)]
    return lax.ppermute(v, "col", perm)


def place(ids, blocks, rows, store):
    y, x, core = ids[1], ids[2], ids[3]
    for other in range(2):
        half = core ^ other
        for k, block in enumerate(blocks[4 * other : 4 * other + 4]):
            for j in range(4):
                along_x = jnp.where(half == 0, x ^ j, x ^ k)
                along_y = jnp.where(half == 0, y ^ k, y ^ j)
                for r in range(2):
                    at = (j * 2 + r) * rows
                    store(half, along_y * 8 + along_x * 2 + (half ^ r), block[at : at + rows, :])


def split(v):
    high = v.astype(BF16)
    return high, (v - high.astype(F32)).astype(BF16)


def dot(a, b):
    return lax.dot_general(a, b, (((1,), (0,)), ((), ())), preferred_element_type=F32)


def dot_full(a, b):
    return lax.dot_general(
        a, b, (((1,), (0,)), ((), ())), precision=lax.Precision.HIGHEST, preferred_element_type=F32
    )


def invert(ids, blocks, top_out, low_out, held):
    odd = jnp.broadcast_to(ids[0] % 2, (8, 128)) == 1

    def store(half, chunk, piece):
        row = pl.multiple_of(chunk * 16 + half * 8, 8)
        for q in range(4):
            lanes = piece[:, 128 * q : 128 * q + 128]
            swapped = jnp.concatenate([lanes[:, 64:], lanes[:, :64]], axis=1)
            held[q ^ (ids[0] // 2), pl.ds(row, 8), :] = jnp.where(odd, swapped, lanes)

    place(ids, blocks, 8, store)

    def part(r, c, n):
        return jnp.concatenate([held[c // 128 + q, r : r + n, :] for q in range(n // 128)], axis=1)

    n = 128
    rows = lax.broadcasted_iota(jnp.int32, (n, n), 0)
    cols = lax.broadcasted_iota(jnp.int32, (n, n), 1)
    in_block = rows // 16 == cols // 16
    diag = [part(n * g, n * g, n) for g in range(4)]
    packed = []
    for d in diag:
        kept = jnp.where(in_block, d, 0.0)
        packed.append(sum(kept[16 * b : 16 * b + 16, :] for b in range(1, 8)) + kept[0:16, :])
    packed = jnp.concatenate(packed, axis=0)
    sub = lax.broadcasted_iota(jnp.int32, (64, n), 0) % 16
    lane = lax.broadcasted_iota(jnp.int32, (64, n), 1) % 16
    inverse = jnp.where(sub == lane, 1.0, 0.0).astype(F32)
    spread = []
    for k in range(16):
        pick = jnp.where(in_block & (rows % 16 == k), 1.0, 0.0).astype(F32)
        spread.append(dot_full(packed, pick))
    for k in range(15, -1, -1):
        factor = spread[k]
        pivot = []
        for g in range(4):
            at = 16 * g + k
            row = inverse[at : at + 1, :] / factor[at : at + 1, :]
            pivot.append(jnp.broadcast_to(row, (16, n)))
        pivot = jnp.concatenate(pivot, axis=0)
        inverse = jnp.where(sub == k, pivot, inverse - jnp.where(sub < k, factor, 0.0) * pivot)
    blocks = []
    for g in range(4):
        tall = jnp.concatenate([inverse[16 * g : 16 * g + 16, :]] * 8, axis=0)
        blocks.append(jnp.where(in_block, tall, 0.0))
    for b in (16, 32, 64):
        off = (rows // (2 * b) == cols // (2 * b)) & (rows // b < cols // b)
        lefts = [dot_full(blocks[g], jnp.where(off, diag[g], 0.0)) for g in range(4)]
        blocks = [blocks[g] - dot_full(lefts[g], blocks[g]) for g in range(4)]
    pairs = []
    for g in (0, 2):
        corner = -dot_full(dot_full(blocks[g], part(n * g, n * g + n, n)), blocks[g + 1])
        top = jnp.concatenate([blocks[g], corner], axis=1)
        low = jnp.concatenate([jnp.zeros_like(corner), blocks[g + 1]], axis=1)
        pairs.append(jnp.concatenate([top, low], axis=0))
    corner = -dot_full(dot_full(pairs[0], part(0, 256, 256)), pairs[1])
    for at, out, m in ((0, top_out, pairs[0]), (768, top_out, corner), (0, low_out, pairs[1])):
        high, low = split(m)
        out[:, at : at + 256] = high
        out[:, at + 256 : at + 512] = high
        out[:, at + 512 : at + 768] = low


def split_tall(trailing, panel, out):
    n = trailing.shape[0]
    side = jnp.concatenate([panel, jnp.zeros((112, n), F32)], axis=0).T
    for v, lanes in ((trailing, slice(0, 384)), (side, slice(384, 512))):
        high, low = split(v)
        out[0:n, lanes] = high
        out[n : 2 * n, lanes] = low
        out[2 * n : 3 * n, lanes] = high


def prepare_kernel(ids, *refs):
    blocks = [whole.at[64 * k : 64 * k + 64] for whole in refs[:2] for k in range(4)]
    trailing, panel, top_out, low_out, tall_out, done_out, held, rows, sems = refs[2:]
    n = TILE
    loads = [
        pltpu.make_async_copy(trailing.at[t * n : t * n + n, :], rows.at[t], sems.at[t]) for t in range(2048 // n)
    ]
    for load in loads:
        load.start()
    done_out[...] = jnp.zeros_like(done_out)
    invert(ids, blocks, top_out, low_out, held)
    for t, load in enumerate(loads):
        load.wait()
        split_tall(rows[t], panel[:, t * n : t * n + n], tall_out.at[3 * n * t : 3 * n * t + 3 * n])


def solve_kernel(ids, *refs):
    blocks = refs[:8]
    inv_top, inv_low, tall = refs[8:11]
    solved_out, own_out, given_out = refs[11:14]
    kept_outs = refs[14:18]
    g, x, xs, total, corner, sems = refs[18:]

    def store(half, chunk, piece):
        high, low = split(piece)
        row = chunk * 16
        row = pl.multiple_of(jnp.where(row < 256, row, row + 512), 16)
        g[half, pl.ds(row, 16), :] = high
        g[half, pl.ds(row + 256, 16), :] = low
        g[half, pl.ds(row + 512, 16), :] = high

    place(ids, blocks, 16, store)
    n = TILE
    own = pl.ds(pl.multiple_of(ids[4] * 16, 16), 16)
    copies = []
    for t in range(2048 // n):
        half, lane = divmod(t * n, 1024)
        slot = t % 2
        for rows, lhs, k in ((slice(0, 256), inv_top, 0), (slice(256, 512), inv_low, 768)):
            part = dot(lhs[...], g[half, k:, lane : lane + n])
            x[t, rows, :] = part
            high, low = split(part)
            xs[slot, rows, 0:n] = high
            xs[slot, rows, n : 2 * n] = high
            xs[slot, rows, 2 * n : 3 * n] = low
        copies.append(pltpu.make_async_copy(x.at[t], solved_out.at[:, t * n : t * n + n], sems.at[t]))
        copies[t].start()
        own_out[:, t * n : t * n + n] = x[t, own, :]
        term = dot(xs[slot], tall[3 * n * t : 3 * n * t + 3 * n, :])
        if t == 0:
            total[...] = term
        else:
            total[...] += term

    corner[...] = jnp.zeros_like(corner)
    summed = total[:, 384:512].T
    for t in range(ROWS):
        corner[t, :, 0:64] = summed[0:8, 64 * t : 64 * t + 64]
        corner[t, :, 64:128] = summed[8:16, 64 * t : 64 * t + 64]
    for j in range(4):
        for first, out, at in ((ids[5], given_out, 72 * j), (ids[0], kept_outs[j], 0)):
            target = first ^ (2 * j)
            out[at : at + 64, :] = total[pl.ds(pl.multiple_of(target * 64, 64), 64), 0:384]
            out[at + 64 : at + 72, :] = corner[target]
    for copy in copies:
        copy.wait()


def trailing_kernel(ids, *refs):
    own_parity, other_parity = refs[:4], refs[4]
    solved, grad, out, rs, x_in, grad_in, result, sems = refs[5:]
    n = TRAILING_TILE
    tiles = 2048 // n
    loads, stores = [], []
    for t in range(tiles):
        loads.append(
            (
                pltpu.make_async_copy(solved.at[:, t * n : t * n + n], x_in.at[t], sems.at[0, t]),
                pltpu.make_async_copy(grad.at[t * n : t * n + n, :], grad_in.at[t], sems.at[1, t]),
            )
        )
        stores.append(pltpu.make_async_copy(result.at[t], out.at[t * n : t * n + n, :], sems.at[2, t]))
        for load in loads[t]:
            load.start()
    for j in range(4):
        for first, piece in ((ids[0], own_parity[j][...]), (ids[5], other_parity[64 * j : 64 * j + 64, :])):
            high, low = split(piece)
            row = (first ^ (2 * j)) * 64
            rs[pl.ds(pl.multiple_of(row, 64), 64), :] = high
            rs[pl.ds(pl.multiple_of(row + 512, 64), 64), :] = low
            rs[pl.ds(pl.multiple_of(row + 1024, 64), 64), :] = high
    for t in range(tiles):
        for load in loads[t]:
            load.wait()
        high, low = split(x_in[t].T)
        result[t] = grad_in[t] - dot(jnp.concatenate([high, high, low], axis=1), rs[...])
        stores[t].start()
    for store in stores:
        store.wait()


TRAILING_TILE = 256
TILE = 512
SMEM = pl.BlockSpec(memory_space=pltpu.SMEM)
VMEM = pl.BlockSpec(memory_space=pltpu.VMEM)
HBM = pl.BlockSpec(memory_space=pltpu.HBM)


def shape(dims, dtype=F32):
    return jax.ShapeDtypeStruct(dims, dtype)


def prepare(ids, blocks, trailing, panel):
    tiles = 2048 // TILE
    return pl.pallas_call(
        prepare_kernel,
        out_shape=[shape((256, 1536), BF16), shape((256, 768), BF16), shape((3 * 2048, 512), BF16), shape((8, 128))],
        in_specs=[SMEM] + [VMEM] * 2 + [HBM, VMEM],
        out_specs=[VMEM] * 4,
        scratch_shapes=[
            pltpu.VMEM((4, B, 128), F32),
            pltpu.VMEM((tiles, TILE, 384), F32),
            pltpu.SemaphoreType.DMA((tiles,)),
        ],
        compiler_params=pltpu.CompilerParams(vmem_limit_bytes=16 * MIB),
        cost_estimate=pl.CostEstimate(flops=4_000_000_000, bytes_accessed=10 * MIB, transcendentals=0),
        name="prepare",
    )(ids, *blocks, trailing, panel)


def solve(ids, blocks, inverse, tall):
    return pl.pallas_call(
        solve_kernel,
        out_shape=[shape((B, 2048)), shape((16, 2048)), shape((288, 384))] + [shape((72, 384))] * 4,
        in_specs=[SMEM] + [VMEM] * 11,
        out_specs=[HBM] + [VMEM] * 6,
        scratch_shapes=[
            pltpu.VMEM((2, 3 * B, 1024), BF16),
            pltpu.VMEM((2048 // TILE, B, TILE), F32),
            pltpu.VMEM((2, B, 3 * TILE), BF16),
            pltpu.VMEM((B, 512), F32),
            pltpu.VMEM((ROWS, 8, 384), F32),
            pltpu.SemaphoreType.DMA((2048 // TILE,)),
        ],
        compiler_params=pltpu.CompilerParams(vmem_limit_bytes=17 * MIB),
        cost_estimate=pl.CostEstimate(flops=6_000_000_000, bytes_accessed=12 * MIB, transcendentals=0),
        name="solve",
    )(ids, *blocks, *inverse, tall)


def trailing_update(ids, pieces, solved, grad):
    n = TRAILING_TILE
    tiles = 2048 // n
    return pl.pallas_call(
        trailing_kernel,
        out_shape=shape((2048, 384)),
        in_specs=[SMEM] + [VMEM] * 5 + [HBM] * 2,
        out_specs=HBM,
        scratch_shapes=[
            pltpu.VMEM((3 * B, 384), BF16),
            pltpu.VMEM((tiles, B, n), F32),
            pltpu.VMEM((tiles, n, 384), F32),
            pltpu.VMEM((tiles, n, 384), F32),
            pltpu.SemaphoreType.DMA((3, tiles)),
        ],
        compiler_params=pltpu.CompilerParams(vmem_limit_bytes=13 * MIB),
        cost_estimate=pl.CostEstimate(flops=4_000_000_000, bytes_accessed=11 * MIB, transcendentals=0),
        name="trailing",
    )(ids, *pieces, solved, grad)


def on_device(
    diag_factor,
    panel_factor,
    row_factor,
    trailing_factor,
    panel_grad,
    diag_grad,
    row_grad,
    trailing_grad,
):
    z = lax.axis_index("row")
    col = lax.axis_index("col")
    core = col % 2
    neighbour = jnp.where(core == 0, z ^ 1, (z - 1 + 2 * (z % 2)) % ROWS)
    ids = jnp.stack([z, col // 8, (col // 2) % 4, core, col, neighbour]).astype(jnp.int32)

    grad = panel_grad.T
    kept = jnp.where(core == 0, grad[:, :1024], grad[:, 1024:])
    given = jnp.where(core == 0, grad[:, 1024:], grad[:, :1024])
    grad_pair = jnp.concatenate([kept, with_sibling(given)], axis=0)
    tile = diag_factor.T
    kept = jnp.where(core == 0, tile[:8], tile[8:])
    given = jnp.where(core == 0, tile[8:], tile[:8])
    tile = jnp.concatenate([kept, with_sibling(given)], axis=0)

    even = [tile] + [with_row_partner(tile, k) for k in (2, 4, 6)]
    grad_pairs = [grad_pair] + [with_col_partner(grad_pair, 0, k) for k in (1, 2, 3)]
    even, grad_pairs = lax.optimization_barrier((even, grad_pairs))
    odd = with_row_partner(jnp.concatenate(even, axis=1), 1)
    grad_quad = jnp.concatenate(grad_pairs, axis=0)
    grad_2 = with_col_partner(grad_quad, 1, 2)
    diag_pair = jnp.concatenate([t for j in range(4) for t in (even[j], odd[:, 64 * j : 64 * j + 64])], axis=1)
    diag_quad = jnp.concatenate([diag_pair] + [with_col_partner(diag_pair, 0, k) for k in (1, 2, 3)], axis=0)
    diag_quad, grad_2 = lax.optimization_barrier((diag_quad, grad_2))
    diag_blocks = [diag_quad] + [with_col_partner(diag_quad, 1, k) for k in (1, 2, 3)]
    later_quad, row_factor, diag_blocks = lax.optimization_barrier((grad_quad, row_factor, diag_blocks))
    grad_far = [with_col_partner(later_quad, 1, 1), grad_2, with_col_partner(later_quad, 1, 3)]
    diag_mine = jnp.concatenate(diag_blocks, axis=0)
    diag_blocks = [diag_mine, with_sibling(diag_mine)]
    quad_swapped = with_sibling(grad_quad)

    row_pieces = [row_factor] + [with_row_partner(row_factor, k) for k in (2, 4, 6)]
    *inverse, tall, ready = prepare(ids, diag_blocks, trailing_factor, panel_factor.T)
    grad_far, row_pieces, _ = lax.optimization_barrier((grad_far, row_pieces, ready))
    row_pieces = row_pieces + [with_neighbour(jnp.concatenate(row_pieces, axis=0))]
    grad_blocks = [grad_quad] + grad_far + [quad_swapped] + [with_sibling(b) for b in grad_far]
    solved, own, given, *kept = solve(ids, grad_blocks, inverse, tall)
    trailing_out = trailing_update(ids, row_pieces, solved, trailing_grad)
    taken = with_neighbour(given)
    taken, trailing_out = lax.optimization_barrier((taken, trailing_out))
    sums = [kept[j] + taken[72 * j : 72 * j + 72] for j in range(4)]
    came = [with_row_partner(sums[j], 2 * j) for j in range(1, 4)]

    total = sums[0] + (came[0] + came[1] + came[2])
    row_out = row_grad - total[0:64, :]
    diag_sum = jnp.concatenate([total[64:72, 0:64], total[64:72, 64:128]], axis=0)
    global_rows = z * 64 + jnp.arange(64)[None, :]
    global_cols = col * 16 + jnp.arange(16)[:, None]
    diag_out = jnp.where(global_rows >= global_cols, diag_grad.T - diag_sum, jnp.float32(0.0))
    return (own.T, trailing_out, row_out, diag_out.T)


def solution(mesh):
    both = P("row", "col")
    return jax.shard_map(
        on_device,
        mesh=mesh,
        in_specs=(both,) * 8,
        out_specs=(both,) * 4,
        check_vma=False,
    )
```

```python
import jax
import jax.numpy as jnp
from jax import lax
from jax.experimental import pallas as pl
from jax.experimental.pallas import tpu as pltpu
from jax.sharding import PartitionSpec as P

F32 = jnp.float32
BF16 = jnp.bfloat16
ROWS = 8
COLS = 32
B = 512
MIB = 1 << 20


def with_row_partner(v, k):
    return lax.ppermute(v, "row", [(i, i ^ k) for i in range(ROWS)])


def with_sibling(v):
    return lax.ppermute(v, "col", [(i, i ^ 1) for i in range(COLS)])


def with_neighbour(v):
    perm = []
    for r in range(ROWS):
        for c in range(COLS):
            to = r ^ 1 if c % 2 == 0 else (r - 1 + 2 * (r % 2)) % ROWS
            perm.append((r * COLS + c, to * COLS + c))
    return lax.ppermute(v, ("row", "col"), perm)


def with_col_partner(v, phase, k):
    shift = {0: 1, 1: 3}
    perm = [(i, i ^ (k << shift[phase ^ (i & 1)])) for i in range(COLS)]
    return lax.ppermute(v, "col", perm)


def place(ids, blocks, rows, store):
    y, x, core = ids[1], ids[2], ids[3]
    for other in range(2):
        half = core ^ other
        for k, block in enumerate(blocks[4 * other : 4 * other + 4]):
            for j in range(4):
                along_x = jnp.where(half == 0, x ^ j, x ^ k)
                along_y = jnp.where(half == 0, y ^ k, y ^ j)
                for r in range(2):
                    at = (j * 2 + r) * rows
                    store(half, along_y * 8 + along_x * 2 + (half ^ r), block[at : at + rows, :])


def split(v):
    high = v.astype(BF16)
    return high, (v - high.astype(F32)).astype(BF16)


def dot(a, b):
    return lax.dot_general(a, b, (((1,), (0,)), ((), ())), preferred_element_type=F32)


def dot_full(a, b):
    return lax.dot_general(
        a, b, (((1,), (0,)), ((), ())), precision=lax.Precision.HIGHEST, preferred_element_type=F32
    )


def invert(ids, blocks, top_out, low_out, held):
    y, x, core = ids[1], ids[2], ids[3]
    odd = jnp.broadcast_to(ids[0] % 2, (8, 128)) == 1
    left = lax.broadcasted_iota(jnp.int32, (8, 128), 1) < 64
    for other in range(2):
        even, rest = blocks[2 * other : 2 * other + 2]
        half = core ^ other
        for m in range(4):
            near = (m ^ (ids[0] // 2)) * 32
            far = (m ^ (ids[5 + other] // 2)) * 32
            for k in range(4):
                for j in range(4):
                    lanes = slice(128 * j, 128 * j + 128)
                    own_parity = even[pl.ds(pl.multiple_of(near + 8 * k, 8), 8), lanes]
                    other_parity = rest[pl.ds(pl.multiple_of(far + 8 * k, 8), 8), lanes]
                    low = jnp.where(odd, other_parity, own_parity)
                    high = jnp.where(odd, own_parity, other_parity)
                    along_x = jnp.where(half == 0, x ^ j, x ^ k)
                    along_y = jnp.where(half == 0, y ^ k, y ^ j)
                    row = (along_y * 8 + along_x * 2 + half) * 16 + half * 8
                    held[m, pl.ds(pl.multiple_of(row, 8), 8), :] = jnp.where(left, low, pltpu.roll(high, 64, 1))
                    row = (along_y * 8 + along_x * 2 + (half ^ 1)) * 16 + half * 8
                    held[m, pl.ds(pl.multiple_of(row, 8), 8), :] = jnp.where(left, pltpu.roll(low, 64, 1), high)

    def part(r, c, n):
        return jnp.concatenate([held[c // 128 + q, r : r + n, :] for q in range(n // 128)], axis=1)

    n = 128
    rows = lax.broadcasted_iota(jnp.int32, (n, n), 0)
    cols = lax.broadcasted_iota(jnp.int32, (n, n), 1)
    in_block = rows // 16 == cols // 16
    diag = [part(n * g, n * g, n) for g in range(4)]
    packed = []
    for d in diag:
        kept = jnp.where(in_block, d, 0.0)
        packed.append(sum(kept[16 * b : 16 * b + 16, :] for b in range(1, 8)) + kept[0:16, :])
    packed = jnp.concatenate(packed, axis=0)
    sub = lax.broadcasted_iota(jnp.int32, (64, n), 0) % 16
    lane = lax.broadcasted_iota(jnp.int32, (64, n), 1) % 16
    inverse = jnp.where(sub == lane, 1.0, 0.0).astype(F32)
    spread = []
    for k in range(16):
        pick = jnp.where(in_block & (rows % 16 == k), 1.0, 0.0).astype(F32)
        spread.append(dot_full(packed, pick))
    for k in range(15, -1, -1):
        factor = spread[k]
        pivot = []
        for g in range(4):
            at = 16 * g + k
            row = inverse[at : at + 1, :] / factor[at : at + 1, :]
            pivot.append(jnp.broadcast_to(row, (16, n)))
        pivot = jnp.concatenate(pivot, axis=0)
        inverse = jnp.where(sub == k, pivot, inverse - jnp.where(sub < k, factor, 0.0) * pivot)
    blocks = []
    for g in range(4):
        tall = jnp.concatenate([inverse[16 * g : 16 * g + 16, :]] * 8, axis=0)
        blocks.append(jnp.where(in_block, tall, 0.0))
    for b in (16, 32, 64):
        off = (rows // (2 * b) == cols // (2 * b)) & (rows // b < cols // b)
        lefts = [dot_full(blocks[g], jnp.where(off, diag[g], 0.0)) for g in range(4)]
        blocks = [blocks[g] - dot_full(lefts[g], blocks[g]) for g in range(4)]
    pairs = []
    for g in (0, 2):
        corner = -dot_full(dot_full(blocks[g], part(n * g, n * g + n, n)), blocks[g + 1])
        top = jnp.concatenate([blocks[g], corner], axis=1)
        low = jnp.concatenate([jnp.zeros_like(corner), blocks[g + 1]], axis=1)
        pairs.append(jnp.concatenate([top, low], axis=0))
    corner = -dot_full(dot_full(pairs[0], part(0, 256, 256)), pairs[1])
    for at, out, m in ((0, top_out, pairs[0]), (768, top_out, corner), (0, low_out, pairs[1])):
        high, low = split(m)
        out[:, at : at + 256] = high
        out[:, at + 256 : at + 512] = high
        out[:, at + 512 : at + 768] = low


def split_tall(trailing, panel, out):
    n = trailing.shape[0]
    side = jnp.concatenate([panel, jnp.zeros((112, n), F32)], axis=0).T
    for v, lanes in ((trailing, slice(0, 384)), (side, slice(384, 512))):
        high, low = split(v)
        out[0:n, lanes] = high
        out[n : 2 * n, lanes] = low
        out[2 * n : 3 * n, lanes] = high


def prepare_kernel(ids, *refs):
    blocks = refs[:4]
    top_out, low_out, done_out, held = refs[4:]
    done_out[...] = jnp.zeros_like(done_out)
    invert(ids, blocks, top_out, low_out, held)


def solve_kernel(ids, *refs):
    blocks = refs[:8]
    inv_top, inv_low, trailing, panel = refs[8:12]
    solved_out, own_out, given_out = refs[13:16]
    kept_outs = refs[16:20]
    g, xs, tall, total, corner = refs[20:]

    def store(half, chunk, piece):
        high, low = split(piece)
        row = chunk * 16
        row = pl.multiple_of(jnp.where(row < 256, row, row + 512), 16)
        g[half, pl.ds(row, 16), :] = high
        g[half, pl.ds(row + 256, 16), :] = low
        g[half, pl.ds(row + 512, 16), :] = high

    place(ids, blocks, 16, store)
    n = TILE
    own = pl.ds(pl.multiple_of(ids[4] * 16, 16), 16)
    for t in range(2048 // n):
        half, lane = divmod(t * n, 1024)
        slot = t % 2
        split_tall(trailing[t * n : t * n + n, :], panel[:, t * n : t * n + n], tall.at[slot])
        for rows, lhs, k in ((slice(0, 256), inv_top, 0), (slice(256, 512), inv_low, 768)):
            part = dot(lhs[...], g[half, k:, lane : lane + n])
            solved_out[rows, t * n : t * n + n] = part
            high, low = split(part)
            xs[slot, rows, 0:n] = high
            xs[slot, rows, n : 2 * n] = high
            xs[slot, rows, 2 * n : 3 * n] = low
        term = dot(xs[slot], tall[slot])
        if t == 0:
            total[...] = term
        else:
            total[...] += term

    own_out[...] = solved_out[own, :]
    corner[...] = jnp.zeros_like(corner)
    summed = total[:, 384:512].T
    for t in range(ROWS):
        corner[t, :, 0:64] = summed[0:8, 64 * t : 64 * t + 64]
        corner[t, :, 64:128] = summed[8:16, 64 * t : 64 * t + 64]
    for j in range(4):
        for first, out, at in ((ids[5], given_out, 72 * j), (ids[0], kept_outs[j], 0)):
            target = first ^ (2 * j)
            out[at : at + 64, :] = total[pl.ds(pl.multiple_of(target * 64, 64), 64), 0:384]
            out[at + 64 : at + 72, :] = corner[target]


def trailing_kernel(ids, *refs):
    own_parity, other_parity = refs[:4], refs[4]
    solved, grad, out, rs = refs[5:]

    @pl.when(pl.program_id(0) == 0)
    def _():
        for j in range(4):
            for first, piece in ((ids[0], own_parity[j][...]), (ids[5], other_parity[64 * j : 64 * j + 64, :])):
                high, low = split(piece)
                row = (first ^ (2 * j)) * 64
                rs[pl.ds(pl.multiple_of(row, 64), 64), :] = high
                rs[pl.ds(pl.multiple_of(row + 512, 64), 64), :] = low
                rs[pl.ds(pl.multiple_of(row + 1024, 64), 64), :] = high

    high, low = split(solved[...].T)
    out[...] = grad[...] - dot(jnp.concatenate([high, high, low], axis=1), rs[...])


TILE = 512
SMEM = pl.BlockSpec(memory_space=pltpu.SMEM)
VMEM = pl.BlockSpec(memory_space=pltpu.VMEM)
HBM = pl.BlockSpec(memory_space=pltpu.HBM)


def shape(dims, dtype=F32):
    return jax.ShapeDtypeStruct(dims, dtype)


def prepare(ids, blocks):
    return pl.pallas_call(
        prepare_kernel,
        out_shape=[shape((256, 1536), BF16), shape((256, 768), BF16), shape((8, 128))],
        in_specs=[SMEM] + [VMEM] * 4,
        out_specs=[VMEM] * 3,
        scratch_shapes=[pltpu.VMEM((4, B, 128), F32)],
        compiler_params=pltpu.CompilerParams(vmem_limit_bytes=8 * MIB),
        cost_estimate=pl.CostEstimate(flops=1_000_000, bytes_accessed=1 << 16, transcendentals=0),
        name="prepare",
    )(ids, *blocks)


def solve(ids, blocks, inverse, trailing, panel, ready):
    return pl.pallas_call(
        solve_kernel,
        out_shape=[shape((B, 2048)), shape((16, 2048)), shape((288, 384))] + [shape((72, 384))] * 4,
        in_specs=[SMEM] + [VMEM] * 13,
        out_specs=[VMEM] * 7,
        scratch_shapes=[
            pltpu.VMEM((2, 3 * B, 1024), BF16),
            pltpu.VMEM((2, B, 3 * TILE), BF16),
            pltpu.VMEM((2, 3 * TILE, 512), BF16),
            pltpu.VMEM((B, 512), F32),
            pltpu.VMEM((ROWS, 8, 384), F32),
        ],
        compiler_params=pltpu.CompilerParams(vmem_limit_bytes=20 * MIB),
        cost_estimate=pl.CostEstimate(flops=6_000_000_000, bytes_accessed=12 * MIB, transcendentals=0),
        name="solve",
    )(ids, *blocks, *inverse, trailing, panel, ready)


def trailing_update(ids, pieces, solved, grad):
    tile = 256
    return pl.pallas_call(
        trailing_kernel,
        grid=(2048 // tile,),
        out_shape=shape((2048, 384)),
        in_specs=[SMEM]
        + [pl.BlockSpec((64, 384), lambda i: (0, 0))] * 4
        + [pl.BlockSpec((256, 384), lambda i: (0, 0))]
        + [pl.BlockSpec((B, tile), lambda i: (0, i)), pl.BlockSpec((tile, 384), lambda i: (i, 0))],
        out_specs=pl.BlockSpec((tile, 384), lambda i: (i, 0)),
        scratch_shapes=[pltpu.VMEM((3 * B, 384), BF16)],
        compiler_params=pltpu.CompilerParams(vmem_limit_bytes=10 * MIB),
        cost_estimate=pl.CostEstimate(flops=4_000_000_000, bytes_accessed=11 * MIB, transcendentals=0),
        name="trailing",
    )(ids, *pieces, solved, grad)


def on_device(
    diag_factor,
    panel_factor,
    row_factor,
    trailing_factor,
    panel_grad,
    diag_grad,
    row_grad,
    trailing_grad,
):
    z = lax.axis_index("row")
    col = lax.axis_index("col")
    core = col % 2
    neighbour = jnp.where(core == 0, z ^ 1, (z - 1 + 2 * (z % 2)) % ROWS)
    other_neighbour = jnp.where(core == 1, z ^ 1, (z - 1 + 2 * (z % 2)) % ROWS)
    ids = jnp.stack([z, col // 8, (col // 2) % 4, core, col, neighbour, other_neighbour]).astype(jnp.int32)

    grad = panel_grad.T
    kept = jnp.where(core == 0, grad[:, :1024], grad[:, 1024:])
    given = jnp.where(core == 0, grad[:, 1024:], grad[:, :1024])
    grad_pair = jnp.concatenate([kept, with_sibling(given)], axis=0)
    tile = diag_factor.T
    kept = jnp.where(core == 0, tile[:8], tile[8:])
    given = jnp.where(core == 0, tile[8:], tile[:8])
    diag_pair = jnp.concatenate([kept, with_sibling(given)], axis=1)

    both = jnp.concatenate([grad_pair, jnp.pad(diag_pair, ((0, 0), (0, 1024 - 128)))], axis=0)
    both = [both] + [with_col_partner(both, 0, k) for k in (1, 2, 3)]
    diag_quad = jnp.concatenate([b[32:, :128] for b in both], axis=1)
    diag_far = [with_col_partner(diag_quad, 1, k) for k in (1, 2, 3)]
    diag_far, both = lax.optimization_barrier((diag_far, both))
    grad_quad = jnp.concatenate([b[:32] for b in both], axis=0)
    grad_far = [with_col_partner(grad_quad, 1, k) for k in (1, 2, 3)]
    diag_even = jnp.concatenate([diag_quad] + diag_far, axis=0)
    diag_even = jnp.concatenate([diag_even] + [with_row_partner(diag_even, k) for k in (2, 4, 6)], axis=0)
    diag_odd = with_neighbour(diag_even)
    row_factor, diag_odd = lax.optimization_barrier((row_factor, diag_odd))
    diag_blocks = [diag_even, diag_odd, with_sibling(diag_even), with_sibling(diag_odd)]
    quad_swapped = with_sibling(grad_quad)

    row_pieces = [row_factor] + [with_row_partner(row_factor, k) for k in (2, 4, 6)]
    *inverse, ready = prepare(ids, diag_blocks)
    grad_far, row_pieces, ready = lax.optimization_barrier((grad_far, row_pieces, ready))
    row_pieces = row_pieces + [with_neighbour(jnp.concatenate(row_pieces, axis=0))]
    grad_blocks = [grad_quad] + grad_far + [quad_swapped] + [with_sibling(b) for b in grad_far]
    solved, own, given, *kept = solve(ids, grad_blocks, inverse, trailing_factor, panel_factor.T, ready)
    trailing_out = trailing_update(ids, row_pieces, solved, trailing_grad)
    taken = with_neighbour(given)
    taken, trailing_out = lax.optimization_barrier((taken, trailing_out))
    sums = [kept[j] + taken[72 * j : 72 * j + 72] for j in range(4)]
    came = [with_row_partner(sums[j], 2 * j) for j in range(1, 4)]

    total = sums[0] + (came[0] + came[1] + came[2])
    row_out = row_grad - total[0:64, :]
    diag_sum = jnp.concatenate([total[64:72, 0:64], total[64:72, 64:128]], axis=0)
    global_rows = z * 64 + jnp.arange(64)[None, :]
    global_cols = col * 16 + jnp.arange(16)[:, None]
    diag_out = jnp.where(global_rows >= global_cols, diag_grad.T - diag_sum, jnp.float32(0.0))
    return (own.T, trailing_out, row_out, diag_out.T)


def solution(mesh):
    both = P("row", "col")
    return jax.shard_map(
        on_device,
        mesh=mesh,
        in_specs=(both,) * 8,
        out_specs=(both,) * 4,
        check_vma=False,
    )
```

```python
import jax
import jax.numpy as jnp
from jax import lax
from jax.experimental import pallas as pl
from jax.experimental.pallas import tpu as pltpu
from jax.sharding import PartitionSpec as P

F32 = jnp.float32
BF16 = jnp.bfloat16
ROWS = 8
COLS = 32
B = 512
MIB = 1 << 20


def with_row_partner(v, k):
    return lax.ppermute(v, "row", [(i, i ^ k) for i in range(ROWS)])


def with_sibling(v):
    return lax.ppermute(v, "col", [(i, i ^ 1) for i in range(COLS)])


def with_neighbour(v):
    perm = []
    for r in range(ROWS):
        for c in range(COLS):
            to = r ^ 1 if c % 2 == 0 else (r - 1 + 2 * (r % 2)) % ROWS
            perm.append((r * COLS + c, to * COLS + c))
    return lax.ppermute(v, ("row", "col"), perm)


def with_col_partner(v, phase, k):
    shift = {0: 1, 1: 3}
    perm = [(i, i ^ (k << shift[phase ^ (i & 1)])) for i in range(COLS)]
    return lax.ppermute(v, "col", perm)


def place(ids, blocks, other, store):
    y, x, half = ids[1], ids[2], ids[3] ^ other
    for k, block in enumerate(blocks):
        for j in range(4):
            along_x = jnp.where(half == 0, x ^ j, x ^ k)
            along_y = jnp.where(half == 0, y ^ k, y ^ j)
            for r in range(2):
                at = (j * 2 + r) * 16
                store((along_y * 8 + along_x * 2 + (half ^ r)) * 16, block[at : at + 16, :])


def split(v):
    high = v.astype(BF16)
    return high, (v - high.astype(F32)).astype(BF16)


def dot(a, b):
    return lax.dot_general(a, b, (((1,), (0,)), ((), ())), preferred_element_type=F32)


def dot_full(a, b):
    return lax.dot_general(
        a, b, (((1,), (0,)), ((), ())), precision=lax.Precision.HIGHEST, preferred_element_type=F32
    )


def invert(ids, blocks, top_out, low_out, held):
    y, x, core = ids[1], ids[2], ids[3]
    odd = jnp.broadcast_to(ids[0] % 2, (8, 128)) == 1
    left = lax.broadcasted_iota(jnp.int32, (8, 128), 1) < 64
    for other in range(2):
        even, rest = blocks[2 * other : 2 * other + 2]
        half = core ^ other
        for m in range(4):
            near = (m ^ (ids[0] // 2)) * 32
            far = (m ^ (ids[5 + other] // 2)) * 32
            for k in range(4):
                for j in range(4):
                    lanes = slice(128 * j, 128 * j + 128)
                    own_parity = even[pl.ds(pl.multiple_of(near + 8 * k, 8), 8), lanes]
                    other_parity = rest[pl.ds(pl.multiple_of(far + 8 * k, 8), 8), lanes]
                    low = jnp.where(odd, other_parity, own_parity)
                    high = jnp.where(odd, own_parity, other_parity)
                    along_x = jnp.where(half == 0, x ^ j, x ^ k)
                    along_y = jnp.where(half == 0, y ^ k, y ^ j)
                    row = (along_y * 8 + along_x * 2 + half) * 16 + half * 8
                    held[m, pl.ds(pl.multiple_of(row, 8), 8), :] = jnp.where(left, low, pltpu.roll(high, 64, 1))
                    row = (along_y * 8 + along_x * 2 + (half ^ 1)) * 16 + half * 8
                    held[m, pl.ds(pl.multiple_of(row, 8), 8), :] = jnp.where(left, pltpu.roll(low, 64, 1), high)

    def part(r, c, n):
        return jnp.concatenate([held[c // 128 + q, r : r + n, :] for q in range(n // 128)], axis=1)

    n = 128
    rows = lax.broadcasted_iota(jnp.int32, (n, n), 0)
    cols = lax.broadcasted_iota(jnp.int32, (n, n), 1)
    in_block = rows // 16 == cols // 16
    diag = [part(n * g, n * g, n) for g in range(4)]
    packed = []
    for d in diag:
        kept = jnp.where(in_block, d, 0.0)
        packed.append(sum(kept[16 * b : 16 * b + 16, :] for b in range(1, 8)) + kept[0:16, :])
    packed = jnp.concatenate(packed, axis=0)
    sub = lax.broadcasted_iota(jnp.int32, (64, n), 0) % 16
    lane = lax.broadcasted_iota(jnp.int32, (64, n), 1) % 16
    inverse = jnp.where(sub == lane, 1.0, 0.0).astype(F32)
    spread = []
    for k in range(16):
        pick = jnp.where(in_block & (rows % 16 == k), 1.0, 0.0).astype(F32)
        spread.append(dot_full(packed, pick))
    for k in range(15, -1, -1):
        factor = spread[k]
        pivot = []
        for g in range(4):
            at = 16 * g + k
            row = inverse[at : at + 1, :] / factor[at : at + 1, :]
            pivot.append(jnp.broadcast_to(row, (16, n)))
        pivot = jnp.concatenate(pivot, axis=0)
        inverse = jnp.where(sub == k, pivot, inverse - jnp.where(sub < k, factor, 0.0) * pivot)
    blocks = []
    for g in range(4):
        tall = jnp.concatenate([inverse[16 * g : 16 * g + 16, :]] * 8, axis=0)
        blocks.append(jnp.where(in_block, tall, 0.0))
    for b in (16, 32, 64):
        off = (rows // (2 * b) == cols // (2 * b)) & (rows // b < cols // b)
        lefts = [dot_full(blocks[g], jnp.where(off, diag[g], 0.0)) for g in range(4)]
        blocks = [blocks[g] - dot_full(lefts[g], blocks[g]) for g in range(4)]
    pairs = []
    for g in (0, 2):
        corner = -dot_full(dot_full(blocks[g], part(n * g, n * g + n, n)), blocks[g + 1])
        top = jnp.concatenate([blocks[g], corner], axis=1)
        low = jnp.concatenate([jnp.zeros_like(corner), blocks[g + 1]], axis=1)
        pairs.append(jnp.concatenate([top, low], axis=0))
    corner = -dot_full(dot_full(pairs[0], part(0, 256, 256)), pairs[1])
    for at, out, m in ((0, top_out, pairs[0]), (768, top_out, corner), (0, low_out, pairs[1])):
        high, low = split(m)
        out[:, at : at + 256] = high
        out[:, at + 256 : at + 512] = high
        out[:, at + 512 : at + 768] = low


def split_tall(trailing, panel, out):
    n = trailing.shape[0]
    side = jnp.concatenate([panel, jnp.zeros((112, n), F32)], axis=0).T
    for v, lanes in ((trailing, slice(0, 384)), (side, slice(384, 512))):
        high, low = split(v)
        out[0:n, lanes] = high
        out[n : 2 * n, lanes] = low
        out[2 * n : 3 * n, lanes] = high


def prepare_kernel(ids, *refs):
    blocks = refs[:4]
    top_out, low_out, held = refs[4:]
    invert(ids, blocks, top_out, low_out, held)


def solve_kernel(ids, *refs):
    blocks = refs[:8]
    inv_top, inv_low, trailing, panel = refs[8:12]
    solved_out, own_out, given_out = refs[12:15]
    kept_outs = refs[15:19]
    g, xs, tall, total, corner = refs[19:]

    n = TILE
    for t in range(2048 // n):
        other, lane = divmod(t * n, 1024)
        if lane == 0:

            def store(row, piece):
                high, low = split(piece)
                row = pl.multiple_of(jnp.where(row < 256, row, row + 512), 16)
                g[other, pl.ds(row, 16), :] = high
                g[other, pl.ds(row + 256, 16), :] = low
                g[other, pl.ds(row + 512, 16), :] = high

            place(ids, blocks[4 * other : 4 * other + 4], other, store)
        slot = t % 2
        here = pl.ds(pl.multiple_of((ids[3] ^ other) * 1024 + lane, n), n)
        split_tall(trailing[here, :], panel[:, here], tall.at[slot])
        for rows, lhs, k in ((slice(0, 256), inv_top, 0), (slice(256, 512), inv_low, 768)):
            part = dot(lhs[...], g[other, k:, lane : lane + n])
            solved_out[rows, here] = part
            high, low = split(part)
            xs[slot, rows, 0:n] = high
            xs[slot, rows, n : 2 * n] = high
            xs[slot, rows, 2 * n : 3 * n] = low
        term = dot(xs[slot], tall[slot])
        if t == 0:
            total[...] = term
        else:
            total[...] += term

    own = pl.ds(pl.multiple_of(ids[4] * 16, 16), 16)
    own_out[...] = solved_out[own, :]
    corner[...] = jnp.zeros_like(corner)
    summed = total[:, 384:512].T
    for t in range(ROWS):
        corner[t, :, 0:64] = summed[0:8, 64 * t : 64 * t + 64]
        corner[t, :, 64:128] = summed[8:16, 64 * t : 64 * t + 64]
    for j in range(4):
        for first, out, at in ((ids[5], given_out, 72 * j), (ids[0], kept_outs[j], 0)):
            target = first ^ (2 * j)
            out[at : at + 64, :] = total[pl.ds(pl.multiple_of(target * 64, 64), 64), 0:384]
            out[at + 64 : at + 72, :] = corner[target]


def trailing_kernel(ids, *refs):
    own_parity, other_parity = refs[:4], refs[4]
    solved, grad, out, rs = refs[5:]

    @pl.when(pl.program_id(0) == 0)
    def _():
        for j in range(4):
            for first, piece in ((ids[0], own_parity[j][...]), (ids[5], other_parity[64 * j : 64 * j + 64, :])):
                high, low = split(piece)
                row = (first ^ (2 * j)) * 64
                rs[pl.ds(pl.multiple_of(row, 64), 64), :] = high
                rs[pl.ds(pl.multiple_of(row + 512, 64), 64), :] = low
                rs[pl.ds(pl.multiple_of(row + 1024, 64), 64), :] = high

    high, low = split(solved[...].T)
    out[...] = grad[...] - dot(jnp.concatenate([high, high, low], axis=1), rs[...])


TILE = 512
SMEM = pl.BlockSpec(memory_space=pltpu.SMEM)
VMEM = pl.BlockSpec(memory_space=pltpu.VMEM)
HBM = pl.BlockSpec(memory_space=pltpu.HBM)


def shape(dims, dtype=F32):
    return jax.ShapeDtypeStruct(dims, dtype)


def prepare(ids, blocks):
    return pl.pallas_call(
        prepare_kernel,
        out_shape=[shape((256, 1536), BF16), shape((256, 768), BF16)],
        in_specs=[SMEM] + [VMEM] * 4,
        out_specs=[VMEM] * 2,
        scratch_shapes=[pltpu.VMEM((4, B, 128), F32)],
        compiler_params=pltpu.CompilerParams(vmem_limit_bytes=8 * MIB),
        cost_estimate=pl.CostEstimate(flops=1_000_000, bytes_accessed=1 << 16, transcendentals=0),
        name="prepare",
    )(ids, *blocks)


def solve(ids, blocks, inverse, trailing, panel):
    return pl.pallas_call(
        solve_kernel,
        out_shape=[shape((B, 2048)), shape((16, 2048)), shape((288, 384))] + [shape((72, 384))] * 4,
        in_specs=[SMEM] + [VMEM] * 12,
        out_specs=[VMEM] * 7,
        scratch_shapes=[
            pltpu.VMEM((2, 3 * B, 1024), BF16),
            pltpu.VMEM((2, B, 3 * TILE), BF16),
            pltpu.VMEM((2, 3 * TILE, 512), BF16),
            pltpu.VMEM((B, 512), F32),
            pltpu.VMEM((ROWS, 8, 384), F32),
        ],
        compiler_params=pltpu.CompilerParams(vmem_limit_bytes=20 * MIB),
        cost_estimate=pl.CostEstimate(flops=6_000_000_000, bytes_accessed=12 * MIB, transcendentals=0),
        name="solve",
    )(ids, *blocks, *inverse, trailing, panel)


def trailing_update(ids, pieces, solved, grad):
    tile = 256
    return pl.pallas_call(
        trailing_kernel,
        grid=(2048 // tile,),
        out_shape=shape((2048, 384)),
        in_specs=[SMEM]
        + [pl.BlockSpec((64, 384), lambda i: (0, 0))] * 4
        + [pl.BlockSpec((256, 384), lambda i: (0, 0))]
        + [pl.BlockSpec((B, tile), lambda i: (0, i)), pl.BlockSpec((tile, 384), lambda i: (i, 0))],
        out_specs=pl.BlockSpec((tile, 384), lambda i: (i, 0)),
        scratch_shapes=[pltpu.VMEM((3 * B, 384), BF16)],
        compiler_params=pltpu.CompilerParams(vmem_limit_bytes=10 * MIB),
        cost_estimate=pl.CostEstimate(flops=4_000_000_000, bytes_accessed=11 * MIB, transcendentals=0),
        name="trailing",
    )(ids, *pieces, solved, grad)


def on_device(
    diag_factor,
    panel_factor,
    row_factor,
    trailing_factor,
    panel_grad,
    diag_grad,
    row_grad,
    trailing_grad,
):
    z = lax.axis_index("row")
    col = lax.axis_index("col")
    core = col % 2
    neighbour = jnp.where(core == 0, z ^ 1, (z - 1 + 2 * (z % 2)) % ROWS)
    other_neighbour = jnp.where(core == 1, z ^ 1, (z - 1 + 2 * (z % 2)) % ROWS)
    ids = jnp.stack([z, col // 8, (col // 2) % 4, core, col, neighbour, other_neighbour]).astype(jnp.int32)

    grad = panel_grad.T
    kept = jnp.where(core == 0, grad[:, :1024], grad[:, 1024:])
    given = jnp.where(core == 0, grad[:, 1024:], grad[:, :1024])
    grad_pair = jnp.concatenate([kept, with_sibling(given)], axis=0)
    tile = diag_factor.T
    kept = jnp.where(core == 0, tile[:8], tile[8:])
    given = jnp.where(core == 0, tile[8:], tile[:8])
    diag_pair = jnp.concatenate([kept, with_sibling(given)], axis=1)

    both = jnp.concatenate([grad_pair, jnp.pad(diag_pair, ((0, 0), (0, 1024 - 128)))], axis=0)
    both = [both] + [with_col_partner(both, 0, k) for k in (1, 2, 3)]
    diag_quad = jnp.concatenate([b[32:, :128] for b in both], axis=1)
    diag_far = [with_col_partner(diag_quad, 1, k) for k in (1, 2, 3)]
    diag_far, both = lax.optimization_barrier((diag_far, both))
    grad_quad = jnp.concatenate([b[:32] for b in both], axis=0)
    grad_far = [with_col_partner(grad_quad, 1, k) for k in (1, 2, 3)]
    diag_even = jnp.concatenate([diag_quad] + diag_far, axis=0)
    diag_even = [diag_even] + [with_row_partner(diag_even, k) for k in (2, 4, 6)]
    diag_even, grad_far[0], grad_far[2] = lax.optimization_barrier((diag_even, grad_far[0], grad_far[2]))
    diag_even = jnp.concatenate(diag_even, axis=0)
    row_factor, diag_even = lax.optimization_barrier((row_factor, diag_even))
    diag_odd = with_neighbour(diag_even)
    diag_blocks = [diag_even, diag_odd, with_sibling(diag_even), with_sibling(diag_odd)]
    quad_swapped = with_sibling(grad_quad)

    row_pieces = [row_factor] + [with_row_partner(row_factor, k) for k in (2, 4, 6)]
    inverse = prepare(ids, diag_blocks)
    row_joined = jnp.concatenate(row_pieces, axis=0)
    panel, row_joined = lax.optimization_barrier((panel_factor.T, row_joined))
    row_pieces = row_pieces + [with_neighbour(row_joined)]
    grad_blocks = [grad_quad] + grad_far + [quad_swapped] + [with_sibling(b) for b in grad_far]
    solved, own, given, *kept = solve(ids, grad_blocks, inverse, trailing_factor, panel)
    trailing_out = trailing_update(ids, row_pieces, solved, trailing_grad)
    taken = with_neighbour(given)
    taken, trailing_out = lax.optimization_barrier((taken, trailing_out))
    sums = [kept[j] + taken[72 * j : 72 * j + 72] for j in range(4)]
    came = [with_row_partner(sums[j], 2 * j) for j in range(1, 4)]

    total = sums[0] + (came[0] + came[1] + came[2])
    row_out = row_grad - total[0:64, :]
    diag_sum = jnp.concatenate([total[64:72, 0:64], total[64:72, 64:128]], axis=0)
    global_rows = z * 64 + jnp.arange(64)[None, :]
    global_cols = col * 16 + jnp.arange(16)[:, None]
    diag_out = jnp.where(global_rows >= global_cols, diag_grad.T - diag_sum, jnp.float32(0.0))
    return (own.T, trailing_out, row_out, diag_out.T)


def solution(mesh):
    both = P("row", "col")
    return jax.shard_map(
        on_device,
        mesh=mesh,
        in_specs=(both,) * 8,
        out_specs=(both,) * 4,
        check_vma=False,
    )
```

```python
import jax
import jax.numpy as jnp
from jax import lax
from jax.experimental import pallas as pl
from jax.experimental.pallas import tpu as pltpu
from jax.sharding import PartitionSpec as P

F32 = jnp.float32
BF16 = jnp.bfloat16
ROWS = 8
COLS = 32
B = 512
MIB = 1 << 20


def with_row_partner(v, k):
    return lax.ppermute(v, "row", [(i, i ^ k) for i in range(ROWS)])


def with_sibling(v):
    return lax.ppermute(v, "col", [(i, i ^ 1) for i in range(COLS)])


def with_neighbour(v):
    perm = []
    for r in range(ROWS):
        for c in range(COLS):
            to = r ^ 1 if c % 2 == 0 else (r - 1 + 2 * (r % 2)) % ROWS
            perm.append((r * COLS + c, to * COLS + c))
    return lax.ppermute(v, ("row", "col"), perm)


def with_col_partner(v, phase, k):
    shift = {0: 1, 1: 3}
    perm = [(i, i ^ (k << shift[phase ^ (i & 1)])) for i in range(COLS)]
    return lax.ppermute(v, "col", perm)


def place(ids, blocks, other, store):
    y, x, half = ids[1], ids[2], ids[3] ^ other
    for k, block in enumerate(blocks):
        for j in range(4):
            along_x = jnp.where(half == 0, x ^ j, x ^ k)
            along_y = jnp.where(half == 0, y ^ k, y ^ j)
            for r in range(2):
                at = (j * 2 + r) * 16
                store((along_y * 8 + along_x * 2 + (half ^ r)) * 16, block[at : at + 16, :])


def split(v):
    high = v.astype(BF16)
    return high, (v - high.astype(F32)).astype(BF16)


def dot(a, b):
    return lax.dot_general(a, b, (((1,), (0,)), ((), ())), preferred_element_type=F32)


def dot_full(a, b):
    return lax.dot_general(
        a, b, (((1,), (0,)), ((), ())), precision=lax.Precision.HIGHEST, preferred_element_type=F32
    )


def invert(ids, blocks, top_out, low_out, held):
    y, x, core = ids[1], ids[2], ids[3]
    odd = jnp.broadcast_to(ids[0] % 2, (8, 128)) == 1
    left = lax.broadcasted_iota(jnp.int32, (8, 128), 1) < 64
    for other in range(2):
        even, rest = blocks[2 * other : 2 * other + 2]
        half = core ^ other
        for m in range(4):
            near = (m ^ (ids[0] // 2)) * 32
            far = (m ^ (ids[5 + other] // 2)) * 32
            for k in range(4):
                for j in range(4):
                    lanes = slice(128 * j, 128 * j + 128)
                    own_parity = even[pl.ds(pl.multiple_of(near + 8 * k, 8), 8), lanes]
                    other_parity = rest[pl.ds(pl.multiple_of(far + 8 * k, 8), 8), lanes]
                    low = jnp.where(odd, other_parity, own_parity)
                    high = jnp.where(odd, own_parity, other_parity)
                    along_x = jnp.where(half == 0, x ^ j, x ^ k)
                    along_y = jnp.where(half == 0, y ^ k, y ^ j)
                    row = (along_y * 8 + along_x * 2 + half) * 16 + half * 8
                    held[m, pl.ds(pl.multiple_of(row, 8), 8), :] = jnp.where(left, low, pltpu.roll(high, 64, 1))
                    row = (along_y * 8 + along_x * 2 + (half ^ 1)) * 16 + half * 8
                    held[m, pl.ds(pl.multiple_of(row, 8), 8), :] = jnp.where(left, pltpu.roll(low, 64, 1), high)

    def part(r, c, n):
        return jnp.concatenate([held[c // 128 + q, r : r + n, :] for q in range(n // 128)], axis=1)

    n = 128
    rows = lax.broadcasted_iota(jnp.int32, (n, n), 0)
    cols = lax.broadcasted_iota(jnp.int32, (n, n), 1)
    in_block = rows // 16 == cols // 16
    diag = [part(n * g, n * g, n) for g in range(4)]
    packed = []
    for d in diag:
        kept = jnp.where(in_block, d, 0.0)
        packed.append(sum(kept[16 * b : 16 * b + 16, :] for b in range(1, 8)) + kept[0:16, :])
    packed = jnp.concatenate(packed, axis=0)
    sub = lax.broadcasted_iota(jnp.int32, (64, n), 0) % 16
    lane = lax.broadcasted_iota(jnp.int32, (64, n), 1) % 16
    inverse = jnp.where(sub == lane, 1.0, 0.0).astype(F32)
    spread = []
    for k in range(16):
        pick = jnp.where(in_block & (rows % 16 == k), 1.0, 0.0).astype(F32)
        spread.append(dot_full(packed, pick))
    for k in range(15, -1, -1):
        factor = spread[k]
        pivot = []
        for g in range(4):
            at = 16 * g + k
            row = inverse[at : at + 1, :] / factor[at : at + 1, :]
            pivot.append(jnp.broadcast_to(row, (16, n)))
        pivot = jnp.concatenate(pivot, axis=0)
        inverse = jnp.where(sub == k, pivot, inverse - jnp.where(sub < k, factor, 0.0) * pivot)
    blocks = []
    for g in range(4):
        tall = jnp.concatenate([inverse[16 * g : 16 * g + 16, :]] * 8, axis=0)
        blocks.append(jnp.where(in_block, tall, 0.0))
    for b in (16, 32, 64):
        off = (rows // (2 * b) == cols // (2 * b)) & (rows // b < cols // b)
        lefts = [dot_full(blocks[g], jnp.where(off, diag[g], 0.0)) for g in range(4)]
        blocks = [blocks[g] - dot_full(lefts[g], blocks[g]) for g in range(4)]
    pairs = []
    for g in (0, 2):
        corner = -dot_full(dot_full(blocks[g], part(n * g, n * g + n, n)), blocks[g + 1])
        top = jnp.concatenate([blocks[g], corner], axis=1)
        low = jnp.concatenate([jnp.zeros_like(corner), blocks[g + 1]], axis=1)
        pairs.append(jnp.concatenate([top, low], axis=0))
    corner = -dot_full(dot_full(pairs[0], part(0, 256, 256)), pairs[1])
    for at, out, m in ((0, top_out, pairs[0]), (768, top_out, corner), (0, low_out, pairs[1])):
        high, low = split(m)
        out[:, at : at + 256] = high
        out[:, at + 256 : at + 512] = high
        out[:, at + 512 : at + 768] = low


def split_tall(trailing, panel, out):
    n = trailing.shape[0]
    side = jnp.concatenate([panel, jnp.zeros((112, n), F32)], axis=0).T
    for v, lanes in ((trailing, slice(0, 384)), (side, slice(384, 512))):
        high, low = split(v)
        out[0:n, lanes] = high
        out[n : 2 * n, lanes] = low
        out[2 * n : 3 * n, lanes] = high


def prepare_kernel(ids, *refs):
    blocks = refs[:4]
    top_out, low_out, held = refs[4:]
    invert(ids, blocks, top_out, low_out, held)


def solve_kernel(ids, *refs):
    blocks = refs[:8]
    inv_top, inv_low, trailing, panel = refs[8:12]
    solved_out, own_out, given_out = refs[12:15]
    kept_outs = refs[15:19]
    g, xs, tall, total, corner = refs[19:]

    n = TILE
    for t in range(2048 // n):
        other, lane = divmod(t * n, 1024)
        if lane == 0:

            def store(row, piece):
                high, low = split(piece)
                row = pl.multiple_of(jnp.where(row < 256, row, row + 512), 16)
                g[other, pl.ds(row, 16), :] = high
                g[other, pl.ds(row + 256, 16), :] = low
                g[other, pl.ds(row + 512, 16), :] = high

            place(ids, blocks[4 * other : 4 * other + 4], other, store)
        slot = t % 2
        here = pl.ds(pl.multiple_of((ids[3] ^ other) * 1024 + lane, n), n)
        split_tall(trailing[here, :], panel[:, here], tall.at[slot])
        for rows, lhs, k in ((slice(0, 256), inv_top, 0), (slice(256, 512), inv_low, 768)):
            part = dot(lhs[...], g[other, k:, lane : lane + n])
            solved_out[rows, here] = part
            high, low = split(part)
            xs[slot, rows, 0:n] = high
            xs[slot, rows, n : 2 * n] = high
            xs[slot, rows, 2 * n : 3 * n] = low
        term = dot(xs[slot], tall[slot])
        if t == 0:
            total[...] = term
        else:
            total[...] += term

    own = pl.ds(pl.multiple_of(ids[4] * 16, 16), 16)
    own_out[...] = solved_out[own, :]
    corner[...] = jnp.zeros_like(corner)
    summed = total[:, 384:512].T
    for t in range(ROWS):
        corner[t, :, 0:64] = summed[0:8, 64 * t : 64 * t + 64]
        corner[t, :, 64:128] = summed[8:16, 64 * t : 64 * t + 64]
    for j in range(4):
        for first, out, at in ((ids[5], given_out, 72 * j), (ids[0], kept_outs[j], 0)):
            target = first ^ (2 * j)
            out[at : at + 64, :] = total[pl.ds(pl.multiple_of(target * 64, 64), 64), 0:384]
            out[at + 64 : at + 72, :] = corner[target]


def trailing_kernel(ids, *refs):
    own_parity, other_parity, solved, grad, out, rs = refs

    @pl.when(pl.program_id(0) == 0)
    def _():
        for j, distance in enumerate((0, 4, 2, 6)):
            for first, pieces in ((ids[0], own_parity), (ids[5], other_parity)):
                piece = pieces[64 * j : 64 * j + 64, :]
                high, low = split(piece)
                row = (first ^ distance) * 64
                rs[pl.ds(pl.multiple_of(row, 64), 64), :] = high
                rs[pl.ds(pl.multiple_of(row + 512, 64), 64), :] = low
                rs[pl.ds(pl.multiple_of(row + 1024, 64), 64), :] = high

    high, low = split(solved[...].T)
    out[...] = grad[...] - dot(jnp.concatenate([high, high, low], axis=1), rs[...])


TILE = 512
SMEM = pl.BlockSpec(memory_space=pltpu.SMEM)
VMEM = pl.BlockSpec(memory_space=pltpu.VMEM)
HBM = pl.BlockSpec(memory_space=pltpu.HBM)


def shape(dims, dtype=F32):
    return jax.ShapeDtypeStruct(dims, dtype)


def prepare(ids, blocks):
    return pl.pallas_call(
        prepare_kernel,
        out_shape=[shape((256, 1536), BF16), shape((256, 768), BF16)],
        in_specs=[SMEM] + [VMEM] * 4,
        out_specs=[VMEM] * 2,
        scratch_shapes=[pltpu.VMEM((4, B, 128), F32)],
        compiler_params=pltpu.CompilerParams(vmem_limit_bytes=8 * MIB),
        cost_estimate=pl.CostEstimate(flops=1_000_000, bytes_accessed=1 << 16, transcendentals=0),
        name="prepare",
    )(ids, *blocks)


def solve(ids, blocks, inverse, trailing, panel):
    return pl.pallas_call(
        solve_kernel,
        out_shape=[shape((B, 2048)), shape((16, 2048)), shape((288, 384))] + [shape((72, 384))] * 4,
        in_specs=[SMEM] + [VMEM] * 12,
        out_specs=[VMEM] * 7,
        scratch_shapes=[
            pltpu.VMEM((2, 3 * B, 1024), BF16),
            pltpu.VMEM((2, B, 3 * TILE), BF16),
            pltpu.VMEM((2, 3 * TILE, 512), BF16),
            pltpu.VMEM((B, 512), F32),
            pltpu.VMEM((ROWS, 8, 384), F32),
        ],
        compiler_params=pltpu.CompilerParams(vmem_limit_bytes=20 * MIB),
        cost_estimate=pl.CostEstimate(flops=6_000_000_000, bytes_accessed=12 * MIB, transcendentals=0),
        name="solve",
    )(ids, *blocks, *inverse, trailing, panel)


def trailing_update(ids, pieces, solved, grad):
    tile = 256
    return pl.pallas_call(
        trailing_kernel,
        grid=(2048 // tile,),
        out_shape=shape((2048, 384)),
        in_specs=[SMEM]
        + [pl.BlockSpec((256, 384), lambda i: (0, 0))] * 2
        + [pl.BlockSpec((B, tile), lambda i: (0, i)), pl.BlockSpec((tile, 384), lambda i: (i, 0))],
        out_specs=pl.BlockSpec((tile, 384), lambda i: (i, 0)),
        scratch_shapes=[pltpu.VMEM((3 * B, 384), BF16)],
        compiler_params=pltpu.CompilerParams(vmem_limit_bytes=10 * MIB),
        cost_estimate=pl.CostEstimate(flops=4_000_000_000, bytes_accessed=11 * MIB, transcendentals=0),
        name="trailing",
    )(ids, *pieces, solved, grad)


def on_device(
    diag_factor,
    panel_factor,
    row_factor,
    trailing_factor,
    panel_grad,
    diag_grad,
    row_grad,
    trailing_grad,
):
    z = lax.axis_index("row")
    col = lax.axis_index("col")
    core = col % 2
    neighbour = jnp.where(core == 0, z ^ 1, (z - 1 + 2 * (z % 2)) % ROWS)
    other_neighbour = jnp.where(core == 1, z ^ 1, (z - 1 + 2 * (z % 2)) % ROWS)
    ids = jnp.stack([z, col // 8, (col // 2) % 4, core, col, neighbour, other_neighbour]).astype(jnp.int32)

    grad = panel_grad.T
    kept = jnp.where(core == 0, grad[:, :1024], grad[:, 1024:])
    given = jnp.where(core == 0, grad[:, 1024:], grad[:, :1024])
    grad_pair = jnp.concatenate([kept, with_sibling(given)], axis=0)
    tile = diag_factor.T
    kept = jnp.where(core == 0, tile[:8], tile[8:])
    given = jnp.where(core == 0, tile[8:], tile[:8])
    diag_pair = jnp.concatenate([kept, with_sibling(given)], axis=1)

    both = jnp.concatenate([grad_pair, jnp.pad(diag_pair, ((0, 0), (0, 1024 - 128)))], axis=0)
    both = [both] + [with_col_partner(both, 0, k) for k in (1, 2, 3)]
    diag_quad = jnp.concatenate([b[32:, :128] for b in both], axis=1)
    row_pair = jnp.concatenate([row_factor, with_row_partner(row_factor, 4)], axis=0)
    row_pair, both = lax.optimization_barrier((row_pair, both))
    row_even = jnp.concatenate([row_pair, with_row_partner(row_pair, 2)], axis=0)
    diag_quad = jnp.concatenate([diag_quad, with_col_partner(diag_quad, 1, 1)], axis=0)
    diag_quad = jnp.concatenate([diag_quad, with_col_partner(diag_quad, 1, 2)], axis=0)
    diag_quad, both, row_even = lax.optimization_barrier((diag_quad, both, row_even))
    row_odd = with_neighbour(row_even)
    grad_quad = jnp.concatenate([b[:32] for b in both], axis=0)
    grad_far = [with_col_partner(grad_quad, 1, k) for k in (1, 2, 3)]
    diag_even = jnp.concatenate([diag_quad, with_row_partner(diag_quad, 2)], axis=0)
    diag_even = jnp.concatenate([diag_even, with_row_partner(diag_even, 4)], axis=0)
    diag_even, row_odd, grad_far[0], grad_far[2] = lax.optimization_barrier(
        (diag_even, row_odd, grad_far[0], grad_far[2])
    )
    diag_odd = with_neighbour(diag_even)
    diag_blocks = [diag_even, diag_odd, with_sibling(diag_even), with_sibling(diag_odd)]
    quad_swapped = with_sibling(grad_quad)

    inverse = prepare(ids, diag_blocks)
    grad_blocks = [grad_quad] + grad_far + [quad_swapped] + [with_sibling(b) for b in grad_far]
    solved, own, given, *kept = solve(ids, grad_blocks, inverse, trailing_factor, panel_factor.T)
    trailing_out = trailing_update(ids, [row_even, row_odd], solved, trailing_grad)
    taken = with_neighbour(given)
    taken, trailing_out = lax.optimization_barrier((taken, trailing_out))
    sums = [kept[j] + taken[72 * j : 72 * j + 72] for j in range(4)]
    came = [with_row_partner(sums[j], 2 * j) for j in range(1, 4)]

    total = sums[0] + (came[0] + came[1] + came[2])
    row_out = row_grad - total[0:64, :]
    diag_sum = jnp.concatenate([total[64:72, 0:64], total[64:72, 64:128]], axis=0)
    global_rows = z * 64 + jnp.arange(64)[None, :]
    global_cols = col * 16 + jnp.arange(16)[:, None]
    diag_out = jnp.where(global_rows >= global_cols, diag_grad.T - diag_sum, jnp.float32(0.0))
    return (own.T, trailing_out, row_out, diag_out.T)


def solution(mesh):
    both = P("row", "col")
    return jax.shard_map(
        on_device,
        mesh=mesh,
        in_specs=(both,) * 8,
        out_specs=(both,) * 4,
        check_vma=False,
    )
```

```python
import jax
import jax.numpy as jnp
from jax import lax
from jax.experimental import pallas as pl
from jax.experimental.pallas import tpu as pltpu
from jax.sharding import PartitionSpec as P

F32 = jnp.float32
BF16 = jnp.bfloat16
ROWS = 8
COLS = 32
B = 512
MIB = 1 << 20


def with_row_partner(v, k):
    return lax.ppermute(v, "row", [(i, i ^ k) for i in range(ROWS)])


def with_sibling(v):
    return lax.ppermute(v, "col", [(i, i ^ 1) for i in range(COLS)])


def with_neighbour(v):
    perm = []
    for r in range(ROWS):
        for c in range(COLS):
            to = r ^ 1 if c % 2 == 0 else (r - 1 + 2 * (r % 2)) % ROWS
            perm.append((r * COLS + c, to * COLS + c))
    return lax.ppermute(v, ("row", "col"), perm)


def with_col_partner(v, phase, k):
    shift = {0: 1, 1: 3}
    perm = [(i, i ^ (k << shift[phase ^ (i & 1)])) for i in range(COLS)]
    return lax.ppermute(v, "col", perm)


def place(ids, blocks, other, store):
    y, x, half = ids[1], ids[2], ids[3] ^ other
    for k, block in enumerate(blocks):
        for j in range(4):
            along_x = jnp.where(half == 0, x ^ j, x ^ k)
            along_y = jnp.where(half == 0, y ^ k, y ^ j)
            for r in range(2):
                at = (j * 2 + r) * 16
                store((along_y * 8 + along_x * 2 + (half ^ r)) * 16, block[at : at + 16, :])


def split(v):
    high = v.astype(BF16)
    return high, (v - high.astype(F32)).astype(BF16)


def dot(a, b):
    return lax.dot_general(a, b, (((1,), (0,)), ((), ())), preferred_element_type=F32)


def dot_full(a, b):
    return lax.dot_general(
        a, b, (((1,), (0,)), ((), ())), precision=lax.Precision.HIGHEST, preferred_element_type=F32
    )


def invert(ids, blocks, top_out, low_out, held):
    y, x, core = ids[1], ids[2], ids[3]
    odd = jnp.broadcast_to(ids[0] % 2, (8, 128)) == 1
    left = lax.broadcasted_iota(jnp.int32, (8, 128), 1) < 64
    for other in range(2):
        even, rest = blocks[2 * other : 2 * other + 2]
        half = core ^ other
        for m in range(4):
            near = (m ^ (ids[0] // 2)) * 32
            far = (m ^ (ids[5 + other] // 2)) * 32
            for k in range(4):
                for j in range(4):
                    lanes = slice(128 * j, 128 * j + 128)
                    own_parity = even[pl.ds(pl.multiple_of(near + 8 * k, 8), 8), lanes]
                    other_parity = rest[pl.ds(pl.multiple_of(far + 8 * k, 8), 8), lanes]
                    low = jnp.where(odd, other_parity, own_parity)
                    high = jnp.where(odd, own_parity, other_parity)
                    along_x = jnp.where(half == 0, x ^ j, x ^ k)
                    along_y = jnp.where(half == 0, y ^ k, y ^ j)
                    row = (along_y * 8 + along_x * 2 + half) * 16 + half * 8
                    held[m, pl.ds(pl.multiple_of(row, 8), 8), :] = jnp.where(left, low, pltpu.roll(high, 64, 1))
                    row = (along_y * 8 + along_x * 2 + (half ^ 1)) * 16 + half * 8
                    held[m, pl.ds(pl.multiple_of(row, 8), 8), :] = jnp.where(left, pltpu.roll(low, 64, 1), high)

    def part(r, c, n):
        return jnp.concatenate([held[c // 128 + q, r : r + n, :] for q in range(n // 128)], axis=1)

    n = 128
    rows = lax.broadcasted_iota(jnp.int32, (n, n), 0)
    cols = lax.broadcasted_iota(jnp.int32, (n, n), 1)
    in_block = rows // 16 == cols // 16
    diag = [part(n * g, n * g, n) for g in range(4)]
    packed = []
    for d in diag:
        kept = jnp.where(in_block, d, 0.0)
        packed.append(sum(kept[16 * b : 16 * b + 16, :] for b in range(1, 8)) + kept[0:16, :])
    packed = jnp.concatenate(packed, axis=0)
    sub = lax.broadcasted_iota(jnp.int32, (64, n), 0) % 16
    lane = lax.broadcasted_iota(jnp.int32, (64, n), 1) % 16
    inverse = jnp.where(sub == lane, 1.0, 0.0).astype(F32)
    spread = []
    for k in range(16):
        pick = jnp.where(in_block & (rows % 16 == k), 1.0, 0.0).astype(F32)
        spread.append(dot_full(packed, pick))
    for k in range(15, -1, -1):
        factor = spread[k]
        pivot = []
        for g in range(4):
            at = 16 * g + k
            row = inverse[at : at + 1, :] / factor[at : at + 1, :]
            pivot.append(jnp.broadcast_to(row, (16, n)))
        pivot = jnp.concatenate(pivot, axis=0)
        inverse = jnp.where(sub == k, pivot, inverse - jnp.where(sub < k, factor, 0.0) * pivot)
    blocks = []
    for g in range(4):
        tall = jnp.concatenate([inverse[16 * g : 16 * g + 16, :]] * 8, axis=0)
        blocks.append(jnp.where(in_block, tall, 0.0))
    for b in (16, 32, 64):
        off = (rows // (2 * b) == cols // (2 * b)) & (rows // b < cols // b)
        lefts = [dot_full(blocks[g], jnp.where(off, diag[g], 0.0)) for g in range(4)]
        blocks = [blocks[g] - dot_full(lefts[g], blocks[g]) for g in range(4)]
    pairs = []
    for g in (0, 2):
        corner = -dot_full(dot_full(blocks[g], part(n * g, n * g + n, n)), blocks[g + 1])
        top = jnp.concatenate([blocks[g], corner], axis=1)
        low = jnp.concatenate([jnp.zeros_like(corner), blocks[g + 1]], axis=1)
        pairs.append(jnp.concatenate([top, low], axis=0))
    corner = -dot_full(dot_full(pairs[0], part(0, 256, 256)), pairs[1])
    for at, out, m in ((0, top_out, pairs[0]), (768, top_out, corner), (0, low_out, pairs[1])):
        high, low = split(m)
        out[:, at : at + 256] = high
        out[:, at + 256 : at + 512] = high
        out[:, at + 512 : at + 768] = low


def split_tall(trailing, panel, out):
    n = trailing.shape[0]
    side = jnp.concatenate([panel, jnp.zeros((112, n), F32)], axis=0).T
    for v, lanes in ((trailing, slice(0, 384)), (side, slice(384, 512))):
        high, low = split(v)
        out[0:n, lanes] = high
        out[n : 2 * n, lanes] = low
        out[2 * n : 3 * n, lanes] = high


def prepare_kernel(ids, *refs):
    blocks = refs[:4]
    top_out, low_out, held = refs[4:]
    invert(ids, blocks, top_out, low_out, held)


def solve_kernel(ids, *refs):
    blocks = refs[:8]
    inv_top, inv_low, trailing, panel = refs[8:12]
    solved_out, own_out, given_out = refs[12:15]
    kept_outs = refs[15:19]
    g, xs, tall, total, corner = refs[19:]

    n = TILE
    for t in range(2048 // n):
        other, lane = divmod(t * n, 1024)
        if lane == 0:

            def store(row, piece):
                high, low = split(piece)
                row = pl.multiple_of(jnp.where(row < 256, row, row + 512), 16)
                g[other, pl.ds(row, 16), :] = high
                g[other, pl.ds(row + 256, 16), :] = low
                g[other, pl.ds(row + 512, 16), :] = high

            place(ids, blocks[4 * other : 4 * other + 4], other, store)
        slot = t % 2
        here = pl.ds(pl.multiple_of((ids[3] ^ other) * 1024 + lane, n), n)
        split_tall(trailing[here, :], panel[:, here], tall.at[slot])
        for rows, lhs, k in ((slice(0, 256), inv_top, 0), (slice(256, 512), inv_low, 768)):
            part = dot(lhs[...], g[other, k:, lane : lane + n])
            solved_out[rows, here] = part
            high, low = split(part)
            xs[slot, rows, 0:n] = high
            xs[slot, rows, n : 2 * n] = high
            xs[slot, rows, 2 * n : 3 * n] = low
        term = dot(xs[slot], tall[slot])
        if t == 0:
            total[...] = term
        else:
            total[...] += term

    own = pl.ds(pl.multiple_of(ids[4] * 16, 16), 16)
    own_out[...] = solved_out[own, :]
    corner[...] = jnp.zeros_like(corner)
    summed = total[:, 384:512].T
    for t in range(ROWS):
        corner[t, :, 0:64] = summed[0:8, 64 * t : 64 * t + 64]
        corner[t, :, 64:128] = summed[8:16, 64 * t : 64 * t + 64]
    for j in range(4):
        for first, out, at in ((ids[5], given_out, 72 * j), (ids[0], kept_outs[j], 0)):
            target = first ^ (2 * j)
            out[at : at + 64, :] = total[pl.ds(pl.multiple_of(target * 64, 64), 64), 0:384]
            out[at + 64 : at + 72, :] = corner[target]


def trailing_kernel(ids, *refs):
    own_parity, other_parity, solved, grad, out, rs = refs

    @pl.when(pl.program_id(0) == 0)
    def _():
        for j, distance in enumerate((0, 4, 2, 6)):
            for first, pieces in ((ids[0], own_parity), (ids[5], other_parity)):
                piece = pieces[64 * j : 64 * j + 64, :]
                high, low = split(piece)
                row = (first ^ distance) * 64
                rs[pl.ds(pl.multiple_of(row, 64), 64), :] = high
                rs[pl.ds(pl.multiple_of(row + 512, 64), 64), :] = low
                rs[pl.ds(pl.multiple_of(row + 1024, 64), 64), :] = high

    high, low = split(solved[...].T)
    out[...] = grad[...] - dot(jnp.concatenate([high, high, low], axis=1), rs[...])


TILE = 512
SMEM = pl.BlockSpec(memory_space=pltpu.SMEM)
VMEM = pl.BlockSpec(memory_space=pltpu.VMEM)
HBM = pl.BlockSpec(memory_space=pltpu.HBM)


def shape(dims, dtype=F32):
    return jax.ShapeDtypeStruct(dims, dtype)


def prepare(ids, blocks):
    return pl.pallas_call(
        prepare_kernel,
        out_shape=[shape((256, 1536), BF16), shape((256, 768), BF16)],
        in_specs=[SMEM] + [VMEM] * 4,
        out_specs=[VMEM] * 2,
        scratch_shapes=[pltpu.VMEM((4, B, 128), F32)],
        compiler_params=pltpu.CompilerParams(vmem_limit_bytes=8 * MIB),
        cost_estimate=pl.CostEstimate(flops=4_000_000_000, bytes_accessed=2 * MIB, transcendentals=0),
        name="prepare",
    )(ids, *blocks)


def solve(ids, blocks, inverse, trailing, panel):
    return pl.pallas_call(
        solve_kernel,
        out_shape=[shape((B, 2048)), shape((16, 2048)), shape((288, 384))] + [shape((72, 384))] * 4,
        in_specs=[SMEM] + [VMEM] * 12,
        out_specs=[VMEM] * 7,
        scratch_shapes=[
            pltpu.VMEM((2, 3 * B, 1024), BF16),
            pltpu.VMEM((2, B, 3 * TILE), BF16),
            pltpu.VMEM((2, 3 * TILE, 512), BF16),
            pltpu.VMEM((B, 512), F32),
            pltpu.VMEM((ROWS, 8, 384), F32),
        ],
        compiler_params=pltpu.CompilerParams(vmem_limit_bytes=20 * MIB),
        cost_estimate=pl.CostEstimate(flops=6_000_000_000, bytes_accessed=12 * MIB, transcendentals=0),
        name="solve",
    )(ids, *blocks, *inverse, trailing, panel)


def trailing_update(ids, pieces, solved, grad):
    tile = 256
    return pl.pallas_call(
        trailing_kernel,
        grid=(2048 // tile,),
        out_shape=shape((2048, 384)),
        in_specs=[SMEM]
        + [pl.BlockSpec((256, 384), lambda i: (0, 0))] * 2
        + [pl.BlockSpec((B, tile), lambda i: (0, i)), pl.BlockSpec((tile, 384), lambda i: (i, 0))],
        out_specs=pl.BlockSpec((tile, 384), lambda i: (i, 0)),
        scratch_shapes=[pltpu.VMEM((3 * B, 384), BF16)],
        compiler_params=pltpu.CompilerParams(vmem_limit_bytes=10 * MIB),
        cost_estimate=pl.CostEstimate(flops=4_000_000_000, bytes_accessed=11 * MIB, transcendentals=0),
        name="trailing",
    )(ids, *pieces, solved, grad)


def on_device(
    diag_factor,
    panel_factor,
    row_factor,
    trailing_factor,
    panel_grad,
    diag_grad,
    row_grad,
    trailing_grad,
):
    z = lax.axis_index("row")
    col = lax.axis_index("col")
    core = col % 2
    neighbour = jnp.where(core == 0, z ^ 1, (z - 1 + 2 * (z % 2)) % ROWS)
    other_neighbour = jnp.where(core == 1, z ^ 1, (z - 1 + 2 * (z % 2)) % ROWS)
    ids = jnp.stack([z, col // 8, (col // 2) % 4, core, col, neighbour, other_neighbour]).astype(jnp.int32)

    grad = panel_grad.T
    kept = jnp.where(core == 0, grad[:, :1024], grad[:, 1024:])
    given = jnp.where(core == 0, grad[:, 1024:], grad[:, :1024])
    grad_pair = jnp.concatenate([kept, with_sibling(given)], axis=0)
    tile = diag_factor.T
    kept = jnp.where(core == 0, tile[:8], tile[8:])
    given = jnp.where(core == 0, tile[8:], tile[:8])
    diag_pair = jnp.concatenate([kept, with_sibling(given)], axis=1)

    both = jnp.concatenate([grad_pair, jnp.pad(diag_pair, ((0, 0), (0, 1024 - 128)))], axis=0)
    both = [both] + [with_col_partner(both, 0, k) for k in (1, 2, 3)]
    diag_quad = jnp.concatenate([b[32:, :128] for b in both], axis=1)
    row_pair = jnp.concatenate([row_factor, with_row_partner(row_factor, 4)], axis=0)
    row_pair, both = lax.optimization_barrier((row_pair, both))
    row_even = jnp.concatenate([row_pair, with_row_partner(row_pair, 2)], axis=0)
    diag_quad = jnp.concatenate([diag_quad, with_col_partner(diag_quad, 1, 1)], axis=0)
    diag_quad = jnp.concatenate([diag_quad, with_col_partner(diag_quad, 1, 2)], axis=0)
    diag_quad, both = lax.optimization_barrier((diag_quad, both))
    grad_quad = jnp.concatenate([b[:32] for b in both], axis=0)
    grad_far = [with_col_partner(grad_quad, 1, k) for k in (1, 2, 3)]
    diag_even = jnp.concatenate([diag_quad, with_row_partner(diag_quad, 2)], axis=0)
    row_even, diag_even = lax.optimization_barrier((row_even, diag_even))
    diag_even = jnp.concatenate([diag_even, with_row_partner(diag_even, 4)], axis=0)
    diag_even, grad_far[0], grad_far[2] = lax.optimization_barrier((diag_even, grad_far[0], grad_far[2]))
    diag_odd = with_neighbour(diag_even)
    row_even, diag_odd = lax.optimization_barrier((row_even, diag_odd))
    row_odd = with_neighbour(row_even)
    diag_blocks = [diag_even, diag_odd, with_sibling(diag_even), with_sibling(diag_odd)]
    quad_swapped = with_sibling(grad_quad)

    inverse = prepare(ids, diag_blocks)
    grad_blocks = [grad_quad] + grad_far + [quad_swapped] + [with_sibling(b) for b in grad_far]
    solved, own, given, *kept = solve(ids, grad_blocks, inverse, trailing_factor, panel_factor.T)
    trailing_out = trailing_update(ids, [row_even, row_odd], solved, trailing_grad)
    taken = with_neighbour(given)
    taken, trailing_out = lax.optimization_barrier((taken, trailing_out))
    sums = [kept[j] + taken[72 * j : 72 * j + 72] for j in range(4)]
    came = [with_row_partner(sums[j], 2 * j) for j in range(1, 4)]

    total = sums[0] + (came[0] + came[1] + came[2])
    row_out = row_grad - total[0:64, :]
    diag_sum = jnp.concatenate([total[64:72, 0:64], total[64:72, 64:128]], axis=0)
    global_rows = z * 64 + jnp.arange(64)[None, :]
    global_cols = col * 16 + jnp.arange(16)[:, None]
    diag_out = jnp.where(global_rows >= global_cols, diag_grad.T - diag_sum, jnp.float32(0.0))
    return (own.T, trailing_out, row_out, diag_out.T)


def solution(mesh):
    both = P("row", "col")
    return jax.shard_map(
        on_device,
        mesh=mesh,
        in_specs=(both,) * 8,
        out_specs=(both,) * 4,
        check_vma=False,
    )
```

```python
import jax
import jax.numpy as jnp
from jax import lax
from jax.experimental import pallas as pl
from jax.experimental.pallas import tpu as pltpu
from jax.sharding import PartitionSpec as P

F32 = jnp.float32
BF16 = jnp.bfloat16
ROWS = 8
COLS = 32
B = 512
MIB = 1 << 20


def with_row_partner(v, k):
    return lax.ppermute(v, "row", [(i, i ^ k) for i in range(ROWS)])


def with_second(v):
    perm = []
    for r in range(ROWS):
        for c in range(COLS):
            perm.append((r * COLS + c, (r ^ (2 if c % 2 == 0 else 6)) * COLS + c))
    return lax.ppermute(v, ("row", "col"), perm)


def with_sibling(v):
    return lax.ppermute(v, "col", [(i, i ^ 1) for i in range(COLS)])


def with_neighbour(v):
    perm = []
    for r in range(ROWS):
        for c in range(COLS):
            to = r ^ 1 if c % 2 == 0 else (r - 1 + 2 * (r % 2)) % ROWS
            perm.append((r * COLS + c, to * COLS + c))
    return lax.ppermute(v, ("row", "col"), perm)


def with_col_partner(v, phase, k):
    shift = {0: 1, 1: 3}
    perm = [(i, i ^ (k << shift[phase ^ (i & 1)])) for i in range(COLS)]
    return lax.ppermute(v, "col", perm)


def place(ids, blocks, other, store):
    y, x, half = ids[1], ids[2], ids[3] ^ other
    for k, block in enumerate(blocks):
        for j in range(4):
            along_x = jnp.where(half == 0, x ^ j, x ^ k)
            along_y = jnp.where(half == 0, y ^ k, y ^ j)
            for r in range(2):
                at = (j * 2 + r) * 16
                store((along_y * 8 + along_x * 2 + (half ^ r)) * 16, block[at : at + 16, :])


def split(v):
    high = v.astype(BF16)
    return high, (v - high.astype(F32)).astype(BF16)


def dot(a, b):
    return lax.dot_general(a, b, (((1,), (0,)), ((), ())), preferred_element_type=F32)


def dot_full(a, b):
    return lax.dot_general(
        a, b, (((1,), (0,)), ((), ())), precision=lax.Precision.HIGHEST, preferred_element_type=F32
    )


def invert(ids, blocks, top_out, low_out, held):
    y, x, core = ids[1], ids[2], ids[3]
    odd = jnp.broadcast_to(ids[0] % 2, (8, 128)) == 1
    left = lax.broadcasted_iota(jnp.int32, (8, 128), 1) < 64
    for other in range(2):
        even, rest = blocks[2 * other : 2 * other + 2]
        half = core ^ other
        for m in range(4):
            near = m ^ (ids[0] // 2)
            near = jnp.where(half == 0, near, (4 - near) % 4) * 32
            far = m ^ (ids[5 + other] // 2)
            far = jnp.where(half == 0, far, (4 - far) % 4) * 32
            for k in range(4):
                for j in range(4):
                    lanes = slice(128 * j, 128 * j + 128)
                    own_parity = even[pl.ds(pl.multiple_of(near + 8 * k, 8), 8), lanes]
                    other_parity = rest[pl.ds(pl.multiple_of(far + 8 * k, 8), 8), lanes]
                    low = jnp.where(odd, other_parity, own_parity)
                    high = jnp.where(odd, own_parity, other_parity)
                    along_x = jnp.where(half == 0, x ^ j, x ^ k)
                    along_y = jnp.where(half == 0, y ^ k, y ^ j)
                    row = (along_y * 8 + along_x * 2 + half) * 16 + half * 8
                    held[m, pl.ds(pl.multiple_of(row, 8), 8), :] = jnp.where(left, low, pltpu.roll(high, 64, 1))
                    row = (along_y * 8 + along_x * 2 + (half ^ 1)) * 16 + half * 8
                    held[m, pl.ds(pl.multiple_of(row, 8), 8), :] = jnp.where(left, pltpu.roll(low, 64, 1), high)

    def part(r, c, n):
        return jnp.concatenate([held[c // 128 + q, r : r + n, :] for q in range(n // 128)], axis=1)

    n = 128
    rows = lax.broadcasted_iota(jnp.int32, (n, n), 0)
    cols = lax.broadcasted_iota(jnp.int32, (n, n), 1)
    in_block = rows // 16 == cols // 16
    diag = [part(n * g, n * g, n) for g in range(4)]
    packed = []
    for d in diag:
        kept = jnp.where(in_block, d, 0.0)
        packed.append(sum(kept[16 * b : 16 * b + 16, :] for b in range(1, 8)) + kept[0:16, :])
    packed = jnp.concatenate(packed, axis=0)
    sub = lax.broadcasted_iota(jnp.int32, (64, n), 0) % 16
    lane = lax.broadcasted_iota(jnp.int32, (64, n), 1) % 16
    inverse = jnp.where(sub == lane, 1.0, 0.0).astype(F32)
    spread = []
    for k in range(16):
        pick = jnp.where(in_block & (rows % 16 == k), 1.0, 0.0).astype(F32)
        spread.append(dot_full(packed, pick))
    for k in range(15, -1, -1):
        factor = spread[k]
        pivot = []
        for g in range(4):
            at = 16 * g + k
            row = inverse[at : at + 1, :] / factor[at : at + 1, :]
            pivot.append(jnp.broadcast_to(row, (16, n)))
        pivot = jnp.concatenate(pivot, axis=0)
        inverse = jnp.where(sub == k, pivot, inverse - jnp.where(sub < k, factor, 0.0) * pivot)
    blocks = []
    for g in range(4):
        tall = jnp.concatenate([inverse[16 * g : 16 * g + 16, :]] * 8, axis=0)
        blocks.append(jnp.where(in_block, tall, 0.0))
    for b in (16, 32, 64):
        off = (rows // (2 * b) == cols // (2 * b)) & (rows // b < cols // b)
        lefts = [dot_full(blocks[g], jnp.where(off, diag[g], 0.0)) for g in range(4)]
        blocks = [blocks[g] - dot_full(lefts[g], blocks[g]) for g in range(4)]
    pairs = []
    for g in (0, 2):
        corner = -dot_full(dot_full(blocks[g], part(n * g, n * g + n, n)), blocks[g + 1])
        top = jnp.concatenate([blocks[g], corner], axis=1)
        low = jnp.concatenate([jnp.zeros_like(corner), blocks[g + 1]], axis=1)
        pairs.append(jnp.concatenate([top, low], axis=0))
    corner = -dot_full(dot_full(pairs[0], part(0, 256, 256)), pairs[1])
    for at, out, m in ((0, top_out, pairs[0]), (768, top_out, corner), (0, low_out, pairs[1])):
        high, low = split(m)
        out[:, at : at + 256] = high
        out[:, at + 256 : at + 512] = high
        out[:, at + 512 : at + 768] = low


def split_tall(trailing, panel, out):
    n = trailing.shape[0]
    side = jnp.concatenate([panel, jnp.zeros((112, n), F32)], axis=0).T
    for v, lanes in ((trailing, slice(0, 384)), (side, slice(384, 512))):
        high, low = split(v)
        out[0:n, lanes] = high
        out[n : 2 * n, lanes] = low
        out[2 * n : 3 * n, lanes] = high


def prepare_kernel(ids, *refs):
    blocks = refs[:4]
    top_out, low_out, held = refs[4:]
    invert(ids, blocks, top_out, low_out, held)


def solve_kernel(ids, *refs):
    blocks = refs[:8]
    inv_top, inv_low, trailing, panel = refs[8:12]
    solved_out, own_out, given_out = refs[12:15]
    kept_outs = refs[15:19]
    g, xs, tall, total, corner = refs[19:]

    n = TILE
    for t in range(2048 // n):
        other, lane = divmod(t * n, 1024)
        if lane == 0:

            def store(row, piece):
                high, low = split(piece)
                row = pl.multiple_of(jnp.where(row < 256, row, row + 512), 16)
                g[other, pl.ds(row, 16), :] = high
                g[other, pl.ds(row + 256, 16), :] = low
                g[other, pl.ds(row + 512, 16), :] = high

            place(ids, blocks[4 * other : 4 * other + 4], other, store)
        slot = t % 2
        here = pl.ds(pl.multiple_of((ids[3] ^ other) * 1024 + lane, n), n)
        split_tall(trailing[here, :], panel[:, here], tall.at[slot])
        for rows, lhs, k in ((slice(0, 256), inv_top, 0), (slice(256, 512), inv_low, 768)):
            part = dot(lhs[...], g[other, k:, lane : lane + n])
            solved_out[rows, here] = part
            high, low = split(part)
            xs[slot, rows, 0:n] = high
            xs[slot, rows, n : 2 * n] = high
            xs[slot, rows, 2 * n : 3 * n] = low
        term = dot(xs[slot], tall[slot])
        if t == 0:
            total[...] = term
        else:
            total[...] += term

    own = pl.ds(pl.multiple_of(ids[4] * 16, 16), 16)
    own_out[...] = solved_out[own, :]
    corner[...] = jnp.zeros_like(corner)
    summed = total[:, 384:512].T
    for t in range(ROWS):
        corner[t, :, 0:64] = summed[0:8, 64 * t : 64 * t + 64]
        corner[t, :, 64:128] = summed[8:16, 64 * t : 64 * t + 64]
    for j in range(4):
        for first, out, at in ((ids[5], given_out, 72 * j), (ids[0], kept_outs[j], 0)):
            target = first ^ (2 * j)
            out[at : at + 64, :] = total[pl.ds(pl.multiple_of(target * 64, 64), 64), 0:384]
            out[at + 64 : at + 72, :] = corner[target]


def trailing_kernel(ids, *refs):
    own_parity, other_parity, solved, grad, out, rs = refs

    @pl.when(pl.program_id(0) == 0)
    def _():
        for j, distance in enumerate((0, 4, 2, 6)):
            distance = distance if j < 2 else jnp.where(ids[3] == 0, distance, 8 - distance)
            for first, pieces in ((ids[0], own_parity), (ids[5], other_parity)):
                piece = pieces[64 * j : 64 * j + 64, :]
                high, low = split(piece)
                row = (first ^ distance) * 64
                rs[pl.ds(pl.multiple_of(row, 64), 64), :] = high
                rs[pl.ds(pl.multiple_of(row + 512, 64), 64), :] = low
                rs[pl.ds(pl.multiple_of(row + 1024, 64), 64), :] = high

    high, low = split(solved[...].T)
    out[...] = grad[...] - dot(jnp.concatenate([high, high, low], axis=1), rs[...])


TILE = 512
SMEM = pl.BlockSpec(memory_space=pltpu.SMEM)
VMEM = pl.BlockSpec(memory_space=pltpu.VMEM)
HBM = pl.BlockSpec(memory_space=pltpu.HBM)


def shape(dims, dtype=F32):
    return jax.ShapeDtypeStruct(dims, dtype)


def prepare(ids, blocks):
    return pl.pallas_call(
        prepare_kernel,
        out_shape=[shape((256, 1536), BF16), shape((256, 768), BF16)],
        in_specs=[SMEM] + [VMEM] * 4,
        out_specs=[VMEM] * 2,
        scratch_shapes=[pltpu.VMEM((4, B, 128), F32)],
        compiler_params=pltpu.CompilerParams(vmem_limit_bytes=8 * MIB),
        cost_estimate=pl.CostEstimate(flops=4_000_000_000, bytes_accessed=2 * MIB, transcendentals=0),
        name="prepare",
    )(ids, *blocks)


def solve(ids, blocks, inverse, trailing, panel):
    return pl.pallas_call(
        solve_kernel,
        out_shape=[shape((B, 2048)), shape((16, 2048)), shape((288, 384))] + [shape((72, 384))] * 4,
        in_specs=[SMEM] + [VMEM] * 12,
        out_specs=[VMEM] * 7,
        scratch_shapes=[
            pltpu.VMEM((2, 3 * B, 1024), BF16),
            pltpu.VMEM((2, B, 3 * TILE), BF16),
            pltpu.VMEM((2, 3 * TILE, 512), BF16),
            pltpu.VMEM((B, 512), F32),
            pltpu.VMEM((ROWS, 8, 384), F32),
        ],
        compiler_params=pltpu.CompilerParams(vmem_limit_bytes=20 * MIB),
        cost_estimate=pl.CostEstimate(flops=6_000_000_000, bytes_accessed=12 * MIB, transcendentals=0),
        name="solve",
    )(ids, *blocks, *inverse, trailing, panel)


def trailing_update(ids, pieces, solved, grad):
    tile = 256
    return pl.pallas_call(
        trailing_kernel,
        grid=(2048 // tile,),
        out_shape=shape((2048, 384)),
        in_specs=[SMEM]
        + [pl.BlockSpec((256, 384), lambda i: (0, 0))] * 2
        + [pl.BlockSpec((B, tile), lambda i: (0, i)), pl.BlockSpec((tile, 384), lambda i: (i, 0))],
        out_specs=pl.BlockSpec((tile, 384), lambda i: (i, 0)),
        scratch_shapes=[pltpu.VMEM((3 * B, 384), BF16)],
        compiler_params=pltpu.CompilerParams(vmem_limit_bytes=10 * MIB),
        cost_estimate=pl.CostEstimate(flops=4_000_000_000, bytes_accessed=11 * MIB, transcendentals=0),
        name="trailing",
    )(ids, *pieces, solved, grad)


def on_device(
    diag_factor,
    panel_factor,
    row_factor,
    trailing_factor,
    panel_grad,
    diag_grad,
    row_grad,
    trailing_grad,
):
    z = lax.axis_index("row")
    col = lax.axis_index("col")
    core = col % 2
    neighbour = jnp.where(core == 0, z ^ 1, (z - 1 + 2 * (z % 2)) % ROWS)
    other_neighbour = jnp.where(core == 1, z ^ 1, (z - 1 + 2 * (z % 2)) % ROWS)
    ids = jnp.stack([z, col // 8, (col // 2) % 4, core, col, neighbour, other_neighbour]).astype(jnp.int32)

    grad = panel_grad.T
    kept = jnp.where(core == 0, grad[:, :1024], grad[:, 1024:])
    given = jnp.where(core == 0, grad[:, 1024:], grad[:, :1024])
    grad_pair = jnp.concatenate([kept, with_sibling(given)], axis=0)
    tile = diag_factor.T
    kept = jnp.where(core == 0, tile[:8], tile[8:])
    given = jnp.where(core == 0, tile[8:], tile[:8])
    diag_pair = jnp.concatenate([kept, with_sibling(given)], axis=1)

    both = jnp.concatenate([grad_pair, jnp.pad(diag_pair, ((0, 0), (0, 1024 - 128)))], axis=0)
    both = [both] + [with_col_partner(both, 0, k) for k in (1, 2, 3)]
    diag_quad = jnp.concatenate([b[32:, :128] for b in both], axis=1)
    diag_quad = jnp.concatenate([diag_quad, with_col_partner(diag_quad, 1, 1)], axis=0)
    diag_quad = jnp.concatenate([diag_quad, with_col_partner(diag_quad, 1, 2)], axis=0)
    row_pair = jnp.concatenate([row_factor, with_row_partner(row_factor, 4)], axis=0)
    diag_quad, both, row_pair = lax.optimization_barrier((diag_quad, both, row_pair))
    grad_quad = jnp.concatenate([b[:32] for b in both], axis=0)
    grad_far = [with_col_partner(grad_quad, 1, k) for k in (1, 2, 3)]
    diag_even = jnp.concatenate([diag_quad, with_second(diag_quad)], axis=0)
    diag_even = jnp.concatenate([diag_even, with_row_partner(diag_even, 4)], axis=0)
    diag_even, row_pair, grad_far[0], grad_far[2] = lax.optimization_barrier(
        (diag_even, row_pair, grad_far[0], grad_far[2])
    )
    diag_odd = with_neighbour(diag_even)
    diag_blocks = [diag_even, diag_odd, with_sibling(diag_even), with_sibling(diag_odd)]
    row_even = jnp.concatenate([row_pair, with_second(row_pair)], axis=0)
    row_odd = with_neighbour(row_even)
    quad_swapped = with_sibling(grad_quad)

    inverse = prepare(ids, diag_blocks)
    grad_blocks = [grad_quad] + grad_far + [quad_swapped] + [with_sibling(b) for b in grad_far]
    solved, own, given, *kept = solve(ids, grad_blocks, inverse, trailing_factor, panel_factor.T)
    trailing_out = trailing_update(ids, [row_even, row_odd], solved, trailing_grad)
    taken = with_neighbour(given)
    taken, trailing_out = lax.optimization_barrier((taken, trailing_out))
    sums = [kept[j] + taken[72 * j : 72 * j + 72] for j in range(4)]
    came = [with_row_partner(sums[j], 2 * j) for j in range(1, 4)]

    total = sums[0] + (came[0] + came[1] + came[2])
    row_out = row_grad - total[0:64, :]
    diag_sum = jnp.concatenate([total[64:72, 0:64], total[64:72, 64:128]], axis=0)
    global_rows = z * 64 + jnp.arange(64)[None, :]
    global_cols = col * 16 + jnp.arange(16)[:, None]
    diag_out = jnp.where(global_rows >= global_cols, diag_grad.T - diag_sum, jnp.float32(0.0))
    return (own.T, trailing_out, row_out, diag_out.T)


def solution(mesh):
    both = P("row", "col")
    return jax.shard_map(
        on_device,
        mesh=mesh,
        in_specs=(both,) * 8,
        out_specs=(both,) * 4,
        check_vma=False,
    )
```

```python
import jax
import jax.numpy as jnp
from jax import lax
from jax.experimental import pallas as pl
from jax.experimental.pallas import tpu as pltpu
from jax.sharding import PartitionSpec as P

F32 = jnp.float32
BF16 = jnp.bfloat16
ROWS = 8
COLS = 32
B = 512
MIB = 1 << 20


def with_row_partner(v, k):
    return lax.ppermute(v, "row", [(i, i ^ k) for i in range(ROWS)])


def with_second(v):
    perm = []
    for r in range(ROWS):
        for c in range(COLS):
            perm.append((r * COLS + c, (r ^ (2 if c % 2 == 0 else 6)) * COLS + c))
    return lax.ppermute(v, ("row", "col"), perm)


def with_sibling(v):
    return lax.ppermute(v, "col", [(i, i ^ 1) for i in range(COLS)])


def with_neighbour(v):
    perm = []
    for r in range(ROWS):
        for c in range(COLS):
            to = r ^ 1 if c % 2 == 0 else (r - 1 + 2 * (r % 2)) % ROWS
            perm.append((r * COLS + c, to * COLS + c))
    return lax.ppermute(v, ("row", "col"), perm)


def with_col_partner(v, phase, k):
    shift = {0: 1, 1: 3}
    perm = [(i, i ^ (k << shift[phase ^ (i & 1)])) for i in range(COLS)]
    return lax.ppermute(v, "col", perm)


def place(ids, blocks, other, store):
    y, x, half = ids[1], ids[2], ids[3] ^ other
    for k, block in enumerate(blocks):
        for j in range(4):
            along_x = jnp.where(half == 0, x ^ j, x ^ k)
            along_y = jnp.where(half == 0, y ^ k, y ^ j)
            for r in range(2):
                at = (j * 2 + r) * 16
                store((along_y * 8 + along_x * 2 + (half ^ r)) * 16, block[at : at + 16, :])


def split(v):
    high = v.astype(BF16)
    return high, (v - high.astype(F32)).astype(BF16)


def dot(a, b):
    return lax.dot_general(a, b, (((1,), (0,)), ((), ())), preferred_element_type=F32)


def dot_full(a, b):
    return lax.dot_general(
        a, b, (((1,), (0,)), ((), ())), precision=lax.Precision.HIGHEST, preferred_element_type=F32
    )


def invert(ids, blocks, top_out, low_out, held):
    y, x, core = ids[1], ids[2], ids[3]
    odd = jnp.broadcast_to(ids[0] % 2, (8, 128)) == 1
    left = lax.broadcasted_iota(jnp.int32, (8, 128), 1) < 64
    for other in range(2):
        even, rest = blocks[2 * other : 2 * other + 2]
        half = core ^ other
        for m in range(4):
            near = m ^ (ids[0] // 2)
            near = jnp.where(half == 0, near, (4 - near) % 4)
            near = (near // 2 + near % 2 * 2) * 32
            far = m ^ (ids[5 + other] // 2)
            far = jnp.where(half == 0, far, (4 - far) % 4)
            far = (far // 2 + far % 2 * 2) * 32
            for k in range(4):
                for j in range(4):
                    lanes = slice(128 * j, 128 * j + 128)
                    own_parity = even[pl.ds(pl.multiple_of(near + 8 * k, 8), 8), lanes]
                    other_parity = rest[pl.ds(pl.multiple_of(far + 8 * k, 8), 8), lanes]
                    low = jnp.where(odd, other_parity, own_parity)
                    high = jnp.where(odd, own_parity, other_parity)
                    along_x = jnp.where(half == 0, x ^ j, x ^ k)
                    along_y = jnp.where(half == 0, y ^ k, y ^ j)
                    row = (along_y * 8 + along_x * 2 + half) * 16 + half * 8
                    held[m, pl.ds(pl.multiple_of(row, 8), 8), :] = jnp.where(left, low, pltpu.roll(high, 64, 1))
                    row = (along_y * 8 + along_x * 2 + (half ^ 1)) * 16 + half * 8
                    held[m, pl.ds(pl.multiple_of(row, 8), 8), :] = jnp.where(left, pltpu.roll(low, 64, 1), high)

    def part(r, c, n):
        return jnp.concatenate([held[c // 128 + q, r : r + n, :] for q in range(n // 128)], axis=1)

    n = 128
    rows = lax.broadcasted_iota(jnp.int32, (n, n), 0)
    cols = lax.broadcasted_iota(jnp.int32, (n, n), 1)
    in_block = rows // 16 == cols // 16
    diag = [part(n * g, n * g, n) for g in range(4)]
    packed = []
    for d in diag:
        kept = jnp.where(in_block, d, 0.0)
        packed.append(sum(kept[16 * b : 16 * b + 16, :] for b in range(1, 8)) + kept[0:16, :])
    packed = jnp.concatenate(packed, axis=0)
    sub = lax.broadcasted_iota(jnp.int32, (64, n), 0) % 16
    lane = lax.broadcasted_iota(jnp.int32, (64, n), 1) % 16
    inverse = jnp.where(sub == lane, 1.0, 0.0).astype(F32)
    spread = []
    for k in range(16):
        pick = jnp.where(in_block & (rows % 16 == k), 1.0, 0.0).astype(F32)
        spread.append(dot_full(packed, pick))
    for k in range(15, -1, -1):
        factor = spread[k]
        pivot = []
        for g in range(4):
            at = 16 * g + k
            row = inverse[at : at + 1, :] / factor[at : at + 1, :]
            pivot.append(jnp.broadcast_to(row, (16, n)))
        pivot = jnp.concatenate(pivot, axis=0)
        inverse = jnp.where(sub == k, pivot, inverse - jnp.where(sub < k, factor, 0.0) * pivot)
    blocks = []
    for g in range(4):
        tall = jnp.concatenate([inverse[16 * g : 16 * g + 16, :]] * 8, axis=0)
        blocks.append(jnp.where(in_block, tall, 0.0))
    for b in (16, 32, 64):
        off = (rows // (2 * b) == cols // (2 * b)) & (rows // b < cols // b)
        lefts = [dot_full(blocks[g], jnp.where(off, diag[g], 0.0)) for g in range(4)]
        blocks = [blocks[g] - dot_full(lefts[g], blocks[g]) for g in range(4)]
    pairs = []
    for g in (0, 2):
        corner = -dot_full(dot_full(blocks[g], part(n * g, n * g + n, n)), blocks[g + 1])
        top = jnp.concatenate([blocks[g], corner], axis=1)
        low = jnp.concatenate([jnp.zeros_like(corner), blocks[g + 1]], axis=1)
        pairs.append(jnp.concatenate([top, low], axis=0))
    corner = -dot_full(dot_full(pairs[0], part(0, 256, 256)), pairs[1])
    for at, out, m in ((0, top_out, pairs[0]), (768, top_out, corner), (0, low_out, pairs[1])):
        high, low = split(m)
        out[:, at : at + 256] = high
        out[:, at + 256 : at + 512] = high
        out[:, at + 512 : at + 768] = low


def split_tall(trailing, panel, out):
    n = trailing.shape[0]
    side = jnp.concatenate([panel, jnp.zeros((112, n), F32)], axis=0).T
    for v, lanes in ((trailing, slice(0, 384)), (side, slice(384, 512))):
        high, low = split(v)
        out[0:n, lanes] = high
        out[n : 2 * n, lanes] = low
        out[2 * n : 3 * n, lanes] = high


def prepare_kernel(ids, *refs):
    blocks = refs[:4]
    top_out, low_out, held = refs[4:]
    invert(ids, blocks, top_out, low_out, held)


def solve_kernel(ids, *refs):
    blocks = refs[:8]
    inv_top, inv_low, trailing, panel = refs[8:12]
    solved_out, own_out, given_out, kept_out = refs[12:16]
    g, xs, tall, total, corner = refs[16:]

    n = TILE
    for t in range(2048 // n):
        other, lane = divmod(t * n, 1024)
        if lane == 0:

            def store(row, piece):
                high, low = split(piece)
                row = pl.multiple_of(jnp.where(row < 256, row, row + 512), 16)
                g[other, pl.ds(row, 16), :] = high
                g[other, pl.ds(row + 256, 16), :] = low
                g[other, pl.ds(row + 512, 16), :] = high

            place(ids, blocks[4 * other : 4 * other + 4], other, store)
        slot = t % 2
        here = pl.ds(pl.multiple_of((ids[3] ^ other) * 1024 + lane, n), n)
        split_tall(trailing[here, :], panel[:, here], tall.at[slot])
        for rows, lhs, k in ((slice(0, 256), inv_top, 0), (slice(256, 512), inv_low, 768)):
            part = dot(lhs[...], g[other, k:, lane : lane + n])
            solved_out[rows, here] = part
            high, low = split(part)
            xs[slot, rows, 0:n] = high
            xs[slot, rows, n : 2 * n] = high
            xs[slot, rows, 2 * n : 3 * n] = low
        term = dot(xs[slot], tall[slot])
        if t == 0:
            total[...] = term
        else:
            total[...] += term

    own = pl.ds(pl.multiple_of(ids[4] * 16, 16), 16)
    own_out[...] = solved_out[own, :]
    corner[...] = jnp.zeros_like(corner)
    summed = total[:, 384:512].T
    for t in range(ROWS):
        corner[t, :, 0:64] = summed[0:8, 64 * t : 64 * t + 64]
        corner[t, :, 64:128] = summed[8:16, 64 * t : 64 * t + 64]
    for j, distance in enumerate((0, 4, 2, 6)):
        distance = distance if j < 2 else jnp.where(ids[3] == 0, distance, 8 - distance)
        at = 72 * j
        for first, out in ((ids[5], given_out), (ids[0], kept_out)):
            target = first ^ distance
            out[at : at + 64, :] = total[pl.ds(pl.multiple_of(target * 64, 64), 64), 0:384]
            out[at + 64 : at + 72, :] = corner[target]


def trailing_kernel(ids, *refs):
    own_parity, other_parity, solved, grad, out, rs = refs

    @pl.when(pl.program_id(0) == 0)
    def _():
        for j, distance in enumerate((0, 4, 2, 6)):
            distance = distance if j < 2 else jnp.where(ids[3] == 0, distance, 8 - distance)
            for first, pieces in ((ids[0], own_parity), (ids[5], other_parity)):
                piece = pieces[64 * j : 64 * j + 64, :]
                high, low = split(piece)
                row = (first ^ distance) * 64
                rs[pl.ds(pl.multiple_of(row, 64), 64), :] = high
                rs[pl.ds(pl.multiple_of(row + 512, 64), 64), :] = low
                rs[pl.ds(pl.multiple_of(row + 1024, 64), 64), :] = high

    high, low = split(solved[...].T)
    out[...] = grad[...] - dot(jnp.concatenate([high, high, low], axis=1), rs[...])


TILE = 512
SMEM = pl.BlockSpec(memory_space=pltpu.SMEM)
VMEM = pl.BlockSpec(memory_space=pltpu.VMEM)
HBM = pl.BlockSpec(memory_space=pltpu.HBM)


def shape(dims, dtype=F32):
    return jax.ShapeDtypeStruct(dims, dtype)


def prepare(ids, blocks):
    return pl.pallas_call(
        prepare_kernel,
        out_shape=[shape((256, 1536), BF16), shape((256, 768), BF16)],
        in_specs=[SMEM] + [VMEM] * 4,
        out_specs=[VMEM] * 2,
        scratch_shapes=[pltpu.VMEM((4, B, 128), F32)],
        compiler_params=pltpu.CompilerParams(vmem_limit_bytes=8 * MIB),
        cost_estimate=pl.CostEstimate(flops=4_000_000_000, bytes_accessed=2 * MIB, transcendentals=0),
        name="prepare",
    )(ids, *blocks)


def solve(ids, blocks, inverse, trailing, panel):
    return pl.pallas_call(
        solve_kernel,
        out_shape=[shape((B, 2048)), shape((16, 2048)), shape((288, 384)), shape((288, 384))],
        in_specs=[SMEM] + [VMEM] * 12,
        out_specs=[VMEM] * 4,
        scratch_shapes=[
            pltpu.VMEM((2, 3 * B, 1024), BF16),
            pltpu.VMEM((2, B, 3 * TILE), BF16),
            pltpu.VMEM((2, 3 * TILE, 512), BF16),
            pltpu.VMEM((B, 512), F32),
            pltpu.VMEM((ROWS, 8, 384), F32),
        ],
        compiler_params=pltpu.CompilerParams(vmem_limit_bytes=20 * MIB),
        cost_estimate=pl.CostEstimate(flops=6_000_000_000, bytes_accessed=12 * MIB, transcendentals=0),
        name="solve",
    )(ids, *blocks, *inverse, trailing, panel)


def trailing_update(ids, pieces, solved, grad):
    tile = 256
    return pl.pallas_call(
        trailing_kernel,
        grid=(2048 // tile,),
        out_shape=shape((2048, 384)),
        in_specs=[SMEM]
        + [pl.BlockSpec((256, 384), lambda i: (0, 0))] * 2
        + [pl.BlockSpec((B, tile), lambda i: (0, i)), pl.BlockSpec((tile, 384), lambda i: (i, 0))],
        out_specs=pl.BlockSpec((tile, 384), lambda i: (i, 0)),
        scratch_shapes=[pltpu.VMEM((3 * B, 384), BF16)],
        compiler_params=pltpu.CompilerParams(vmem_limit_bytes=10 * MIB),
        cost_estimate=pl.CostEstimate(flops=4_000_000_000, bytes_accessed=11 * MIB, transcendentals=0),
        name="trailing",
    )(ids, *pieces, solved, grad)


def on_device(
    diag_factor,
    panel_factor,
    row_factor,
    trailing_factor,
    panel_grad,
    diag_grad,
    row_grad,
    trailing_grad,
):
    z = lax.axis_index("row")
    col = lax.axis_index("col")
    core = col % 2
    neighbour = jnp.where(core == 0, z ^ 1, (z - 1 + 2 * (z % 2)) % ROWS)
    other_neighbour = jnp.where(core == 1, z ^ 1, (z - 1 + 2 * (z % 2)) % ROWS)
    ids = jnp.stack([z, col // 8, (col // 2) % 4, core, col, neighbour, other_neighbour]).astype(jnp.int32)

    grad = panel_grad.T
    kept = jnp.where(core == 0, grad[:, :1024], grad[:, 1024:])
    given = jnp.where(core == 0, grad[:, 1024:], grad[:, :1024])
    grad_pair = jnp.concatenate([kept, with_sibling(given)], axis=0)
    tile = diag_factor.T
    kept = jnp.where(core == 0, tile[:8], tile[8:])
    given = jnp.where(core == 0, tile[8:], tile[:8])
    diag_pair = jnp.concatenate([kept, with_sibling(given)], axis=1)

    both = jnp.concatenate([grad_pair, jnp.pad(diag_pair, ((0, 0), (0, 1024 - 128)))], axis=0)
    both = [both] + [with_col_partner(both, 0, k) for k in (1, 2, 3)]
    row_pair = jnp.concatenate([row_factor, with_row_partner(row_factor, 4)], axis=0)
    both, row_pair = lax.optimization_barrier((both, row_pair))
    diag_quad = jnp.concatenate([b[32:, :128] for b in both], axis=1)
    diag_quad = jnp.concatenate([diag_quad, with_col_partner(diag_quad, 1, 1)], axis=0)
    diag_quad = jnp.concatenate([diag_quad, with_col_partner(diag_quad, 1, 2)], axis=0)
    diag_quad, both = lax.optimization_barrier((diag_quad, both))
    grad_quad = jnp.concatenate([b[:32] for b in both], axis=0)
    grad_far = [with_col_partner(grad_quad, 1, k) for k in (1, 2, 3)]
    diag_even = jnp.concatenate([diag_quad, with_row_partner(diag_quad, 4)], axis=0)
    diag_even = jnp.concatenate([diag_even, with_second(diag_even)], axis=0)
    diag_even, row_pair, grad_far[0], grad_far[2] = lax.optimization_barrier(
        (diag_even, row_pair, grad_far[0], grad_far[2])
    )
    diag_odd = with_neighbour(diag_even)
    diag_blocks = [diag_even, diag_odd, with_sibling(diag_even), with_sibling(diag_odd)]
    row_even = jnp.concatenate([row_pair, with_second(row_pair)], axis=0)
    row_odd = with_neighbour(row_even)
    quad_swapped = with_sibling(grad_quad)

    inverse = prepare(ids, diag_blocks)
    grad_blocks = [grad_quad] + grad_far + [quad_swapped] + [with_sibling(b) for b in grad_far]
    solved, own, given, kept = solve(ids, grad_blocks, inverse, trailing_factor, panel_factor.T)
    trailing_out = trailing_update(ids, [row_even, row_odd], solved, trailing_grad)
    taken = with_neighbour(given)
    taken, trailing_out = lax.optimization_barrier((taken, trailing_out))
    stays = kept[:144] + taken[:144]
    stays = stays + with_second(kept[144:] + taken[144:])
    total = stays[:72] + with_row_partner(stays[72:], 4)
    row_out = row_grad - total[0:64, :]
    diag_sum = jnp.concatenate([total[64:72, 0:64], total[64:72, 64:128]], axis=0)
    global_rows = z * 64 + jnp.arange(64)[None, :]
    global_cols = col * 16 + jnp.arange(16)[:, None]
    diag_out = jnp.where(global_rows >= global_cols, diag_grad.T - diag_sum, jnp.float32(0.0))
    return (own.T, trailing_out, row_out, diag_out.T)


def solution(mesh):
    both = P("row", "col")
    return jax.shard_map(
        on_device,
        mesh=mesh,
        in_specs=(both,) * 8,
        out_specs=(both,) * 4,
        check_vma=False,
    )
```

```python
import jax
import jax.numpy as jnp
from jax import lax
from jax.experimental import pallas as pl
from jax.experimental.pallas import tpu as pltpu
from jax.sharding import PartitionSpec as P

F32 = jnp.float32
BF16 = jnp.bfloat16
ROWS = 8
COLS = 32
B = 512
MIB = 1 << 20


def with_row_partner(v, k):
    return lax.ppermute(v, "row", [(i, i ^ k) for i in range(ROWS)])


def with_second(v):
    perm = []
    for r in range(ROWS):
        for c in range(COLS):
            perm.append((r * COLS + c, (r ^ (2 if c % 2 == 0 else 6)) * COLS + c))
    return lax.ppermute(v, ("row", "col"), perm)


def with_sibling(v):
    return lax.ppermute(v, "col", [(i, i ^ 1) for i in range(COLS)])


def with_neighbour(v):
    perm = []
    for r in range(ROWS):
        for c in range(COLS):
            to = r ^ 1 if c % 2 == 0 else (r - 1 + 2 * (r % 2)) % ROWS
            perm.append((r * COLS + c, to * COLS + c))
    return lax.ppermute(v, ("row", "col"), perm)


def with_col_partner(v, phase, k):
    shift = {0: 1, 1: 3}
    perm = [(i, i ^ (k << shift[phase ^ (i & 1)])) for i in range(COLS)]
    return lax.ppermute(v, "col", perm)


def place(ids, blocks, other, store):
    y, x, half = ids[1], ids[2], ids[3] ^ other
    for k, block in enumerate(blocks):
        for j in range(4):
            along_x = jnp.where(half == 0, x ^ j, x ^ k)
            along_y = jnp.where(half == 0, y ^ k, y ^ j)
            for r in range(2):
                at = (j * 2 + r) * 16
                store((along_y * 8 + along_x * 2 + (half ^ r)) * 16, block[at : at + 16, :])


def split(v):
    high = v.astype(BF16)
    return high, (v - high.astype(F32)).astype(BF16)


def dot(a, b):
    return lax.dot_general(a, b, (((1,), (0,)), ((), ())), preferred_element_type=F32)


def dot_full(a, b):
    return lax.dot_general(
        a, b, (((1,), (0,)), ((), ())), precision=lax.Precision.HIGHEST, preferred_element_type=F32
    )


def invert(ids, blocks, top_out, low_out, held):
    y, x, core = ids[1], ids[2], ids[3]
    odd = jnp.broadcast_to(ids[0] % 2, (8, 128)) == 1
    left = lax.broadcasted_iota(jnp.int32, (8, 128), 1) < 64
    for other in range(2):
        even, rest = blocks[2 * other : 2 * other + 2]
        half = core ^ other
        for m in range(4):
            near = m ^ (ids[0] // 2)
            near = jnp.where(half == 0, near, (4 - near) % 4) * 32
            far = m ^ (ids[5 + other] // 2)
            far = jnp.where(half == 0, far, (4 - far) % 4) * 32
            for k in range(4):
                for j in range(4):
                    lanes = slice(128 * j, 128 * j + 128)
                    own_parity = even[pl.ds(pl.multiple_of(near + 8 * k, 8), 8), lanes]
                    other_parity = rest[pl.ds(pl.multiple_of(far + 8 * k, 8), 8), lanes]
                    low = jnp.where(odd, other_parity, own_parity)
                    high = jnp.where(odd, own_parity, other_parity)
                    along_x = jnp.where(half == 0, x ^ j, x ^ k)
                    along_y = jnp.where(half == 0, y ^ k, y ^ j)
                    row = (along_y * 8 + along_x * 2 + half) * 16 + half * 8
                    held[m, pl.ds(pl.multiple_of(row, 8), 8), :] = jnp.where(left, low, pltpu.roll(high, 64, 1))
                    row = (along_y * 8 + along_x * 2 + (half ^ 1)) * 16 + half * 8
                    held[m, pl.ds(pl.multiple_of(row, 8), 8), :] = jnp.where(left, pltpu.roll(low, 64, 1), high)

    def part(r, c, n):
        return jnp.concatenate([held[c // 128 + q, r : r + n, :] for q in range(n // 128)], axis=1)

    n = 128
    rows = lax.broadcasted_iota(jnp.int32, (n, n), 0)
    cols = lax.broadcasted_iota(jnp.int32, (n, n), 1)
    in_block = rows // 16 == cols // 16
    diag = [part(n * g, n * g, n) for g in range(4)]
    packed = []
    for d in diag:
        kept = jnp.where(in_block, d, 0.0)
        packed.append(sum(kept[16 * b : 16 * b + 16, :] for b in range(1, 8)) + kept[0:16, :])
    packed = jnp.concatenate(packed, axis=0)
    sub = lax.broadcasted_iota(jnp.int32, (64, n), 0) % 16
    lane = lax.broadcasted_iota(jnp.int32, (64, n), 1) % 16
    inverse = jnp.where(sub == lane, 1.0, 0.0).astype(F32)
    spread = []
    for k in range(16):
        pick = jnp.where(in_block & (rows % 16 == k), 1.0, 0.0).astype(F32)
        spread.append(dot_full(packed, pick))
    for k in range(15, -1, -1):
        factor = spread[k]
        pivot = []
        for g in range(4):
            at = 16 * g + k
            row = inverse[at : at + 1, :] / factor[at : at + 1, :]
            pivot.append(jnp.broadcast_to(row, (16, n)))
        pivot = jnp.concatenate(pivot, axis=0)
        inverse = jnp.where(sub == k, pivot, inverse - jnp.where(sub < k, factor, 0.0) * pivot)
    blocks = []
    for g in range(4):
        tall = jnp.concatenate([inverse[16 * g : 16 * g + 16, :]] * 8, axis=0)
        blocks.append(jnp.where(in_block, tall, 0.0))
    for b in (16, 32, 64):
        off = (rows // (2 * b) == cols // (2 * b)) & (rows // b < cols // b)
        lefts = [dot_full(blocks[g], jnp.where(off, diag[g], 0.0)) for g in range(4)]
        blocks = [blocks[g] - dot_full(lefts[g], blocks[g]) for g in range(4)]
    pairs = []
    for g in (0, 2):
        corner = -dot_full(dot_full(blocks[g], part(n * g, n * g + n, n)), blocks[g + 1])
        top = jnp.concatenate([blocks[g], corner], axis=1)
        low = jnp.concatenate([jnp.zeros_like(corner), blocks[g + 1]], axis=1)
        pairs.append(jnp.concatenate([top, low], axis=0))
    corner = -dot_full(dot_full(pairs[0], part(0, 256, 256)), pairs[1])
    for at, out, m in ((0, top_out, pairs[0]), (768, top_out, corner), (0, low_out, pairs[1])):
        high, low = split(m)
        out[:, at : at + 256] = high
        out[:, at + 256 : at + 512] = high
        out[:, at + 512 : at + 768] = low


def split_tall(trailing, panel, out):
    n = trailing.shape[0]
    side = jnp.concatenate([panel, jnp.zeros((112, n), F32)], axis=0).T
    for v, lanes in ((trailing, slice(0, 384)), (side, slice(384, 512))):
        high, low = split(v)
        out[0:n, lanes] = high
        out[n : 2 * n, lanes] = low
        out[2 * n : 3 * n, lanes] = high


def prepare_kernel(ids, *refs):
    blocks = refs[:4]
    top_out, low_out, held = refs[4:]
    invert(ids, blocks, top_out, low_out, held)


def solve_kernel(ids, *refs):
    blocks = refs[:8]
    inv_top, inv_low, trailing, panel = refs[8:12]
    solved_out, own_out, given_out = refs[12:15]
    kept_outs = refs[15:19]
    g, xs, tall, total, corner = refs[19:]

    n = TILE
    for t in range(2048 // n):
        other, lane = divmod(t * n, 1024)
        if lane == 0:

            def store(row, piece):
                high, low = split(piece)
                row = pl.multiple_of(jnp.where(row < 256, row, row + 512), 16)
                g[other, pl.ds(row, 16), :] = high
                g[other, pl.ds(row + 256, 16), :] = low
                g[other, pl.ds(row + 512, 16), :] = high

            place(ids, blocks[4 * other : 4 * other + 4], other, store)
        slot = t % 2
        here = pl.ds(pl.multiple_of((ids[3] ^ other) * 1024 + lane, n), n)
        split_tall(trailing[here, :], panel[:, here], tall.at[slot])
        for rows, lhs, k in ((slice(0, 256), inv_top, 0), (slice(256, 512), inv_low, 768)):
            part = dot(lhs[...], g[other, k:, lane : lane + n])
            solved_out[rows, here] = part
            high, low = split(part)
            xs[slot, rows, 0:n] = high
            xs[slot, rows, n : 2 * n] = high
            xs[slot, rows, 2 * n : 3 * n] = low
        term = dot(xs[slot], tall[slot])
        if t == 0:
            total[...] = term
        else:
            total[...] += term

    own = pl.ds(pl.multiple_of(ids[4] * 16, 16), 16)
    own_out[...] = solved_out[own, :]
    corner[...] = jnp.zeros_like(corner)
    summed = total[:, 384:512].T
    for t in range(ROWS):
        corner[t, :, 0:64] = summed[0:8, 64 * t : 64 * t + 64]
        corner[t, :, 64:128] = summed[8:16, 64 * t : 64 * t + 64]
    for j in range(4):
        for first, out, at in ((ids[5], given_out, 72 * j), (ids[0], kept_outs[j], 0)):
            target = first ^ (2 * j)
            out[at : at + 64, :] = total[pl.ds(pl.multiple_of(target * 64, 64), 64), 0:384]
            out[at + 64 : at + 72, :] = corner[target]


def trailing_kernel(ids, *refs):
    own_parity, other_parity, solved, grad, out, rs = refs

    @pl.when(pl.program_id(0) == 0)
    def _():
        for j, distance in enumerate((0, 4, 2, 6)):
            distance = distance if j < 2 else jnp.where(ids[3] == 0, distance, 8 - distance)
            for first, pieces in ((ids[0], own_parity), (ids[5], other_parity)):
                piece = pieces[64 * j : 64 * j + 64, :]
                high, low = split(piece)
                row = (first ^ distance) * 64
                rs[pl.ds(pl.multiple_of(row, 64), 64), :] = high
                rs[pl.ds(pl.multiple_of(row + 512, 64), 64), :] = low
                rs[pl.ds(pl.multiple_of(row + 1024, 64), 64), :] = high

    high, low = split(solved[...].T)
    out[...] = grad[...] - dot(jnp.concatenate([high, high, low], axis=1), rs[...])


TILE = 512
SMEM = pl.BlockSpec(memory_space=pltpu.SMEM)
VMEM = pl.BlockSpec(memory_space=pltpu.VMEM)
HBM = pl.BlockSpec(memory_space=pltpu.HBM)


def shape(dims, dtype=F32):
    return jax.ShapeDtypeStruct(dims, dtype)


def prepare(ids, blocks):
    return pl.pallas_call(
        prepare_kernel,
        out_shape=[shape((256, 1536), BF16), shape((256, 768), BF16)],
        in_specs=[SMEM] + [VMEM] * 4,
        out_specs=[VMEM] * 2,
        scratch_shapes=[pltpu.VMEM((4, B, 128), F32)],
        compiler_params=pltpu.CompilerParams(vmem_limit_bytes=8 * MIB),
        cost_estimate=pl.CostEstimate(flops=4_000_000_000, bytes_accessed=2 * MIB, transcendentals=0),
        name="prepare",
    )(ids, *blocks)


def solve(ids, blocks, inverse, trailing, panel):
    return pl.pallas_call(
        solve_kernel,
        out_shape=[shape((B, 2048)), shape((16, 2048)), shape((288, 384))] + [shape((72, 384))] * 4,
        in_specs=[SMEM] + [VMEM] * 12,
        out_specs=[VMEM] * 7,
        scratch_shapes=[
            pltpu.VMEM((2, 3 * B, 1024), BF16),
            pltpu.VMEM((2, B, 3 * TILE), BF16),
            pltpu.VMEM((2, 3 * TILE, 512), BF16),
            pltpu.VMEM((B, 512), F32),
            pltpu.VMEM((ROWS, 8, 384), F32),
        ],
        compiler_params=pltpu.CompilerParams(vmem_limit_bytes=20 * MIB),
        cost_estimate=pl.CostEstimate(flops=6_000_000_000, bytes_accessed=12 * MIB, transcendentals=0),
        name="solve",
    )(ids, *blocks, *inverse, trailing, panel)


def trailing_update(ids, pieces, solved, grad):
    tile = 256
    return pl.pallas_call(
        trailing_kernel,
        grid=(2048 // tile,),
        out_shape=shape((2048, 384)),
        in_specs=[SMEM]
        + [pl.BlockSpec((256, 384), lambda i: (0, 0))] * 2
        + [pl.BlockSpec((B, tile), lambda i: (0, i)), pl.BlockSpec((tile, 384), lambda i: (i, 0))],
        out_specs=pl.BlockSpec((tile, 384), lambda i: (i, 0)),
        scratch_shapes=[pltpu.VMEM((3 * B, 384), BF16)],
        compiler_params=pltpu.CompilerParams(vmem_limit_bytes=10 * MIB),
        cost_estimate=pl.CostEstimate(flops=4_000_000_000, bytes_accessed=11 * MIB, transcendentals=0),
        name="trailing",
    )(ids, *pieces, solved, grad)


def on_device(
    diag_factor,
    panel_factor,
    row_factor,
    trailing_factor,
    panel_grad,
    diag_grad,
    row_grad,
    trailing_grad,
):
    z = lax.axis_index("row")
    col = lax.axis_index("col")
    core = col % 2
    neighbour = jnp.where(core == 0, z ^ 1, (z - 1 + 2 * (z % 2)) % ROWS)
    other_neighbour = jnp.where(core == 1, z ^ 1, (z - 1 + 2 * (z % 2)) % ROWS)
    ids = jnp.stack([z, col // 8, (col // 2) % 4, core, col, neighbour, other_neighbour]).astype(jnp.int32)

    grad = panel_grad.T
    kept = jnp.where(core == 0, grad[:, :1024], grad[:, 1024:])
    given = jnp.where(core == 0, grad[:, 1024:], grad[:, :1024])
    grad_pair = jnp.concatenate([kept, with_sibling(given)], axis=0)
    tile = diag_factor.T
    kept = jnp.where(core == 0, tile[:8], tile[8:])
    given = jnp.where(core == 0, tile[8:], tile[:8])
    diag_pair = jnp.concatenate([kept, with_sibling(given)], axis=1)

    both = jnp.concatenate([grad_pair, jnp.pad(diag_pair, ((0, 0), (0, 1024 - 128)))], axis=0)
    both = [both] + [with_col_partner(both, 0, k) for k in (1, 2, 3)]
    diag_quad = jnp.concatenate([b[32:, :128] for b in both], axis=1)
    diag_quad = jnp.concatenate([diag_quad, with_col_partner(diag_quad, 1, 1)], axis=0)
    diag_quad = jnp.concatenate([diag_quad, with_col_partner(diag_quad, 1, 2)], axis=0)
    row_pair = jnp.concatenate([row_factor, with_row_partner(row_factor, 4)], axis=0)
    diag_even = jnp.concatenate([diag_quad, with_second(diag_quad)], axis=0)
    diag_even, both, row_pair = lax.optimization_barrier((diag_even, both, row_pair))
    grad_quad = jnp.concatenate([b[:32] for b in both], axis=0)
    grad_far = [with_col_partner(grad_quad, 1, k) for k in (1, 2, 3)]
    diag_even = jnp.concatenate([diag_even, with_row_partner(diag_even, 4)], axis=0)
    diag_even, row_pair = lax.optimization_barrier((diag_even, row_pair))
    diag_odd = with_neighbour(diag_even)
    diag_odd, grad_far[0], grad_far[2] = lax.optimization_barrier((diag_odd, grad_far[0], grad_far[2]))
    diag_blocks = [diag_even, diag_odd, with_sibling(diag_even), with_sibling(diag_odd)]
    row_even = jnp.concatenate([row_pair, with_second(row_pair)], axis=0)
    row_odd = with_neighbour(row_even)
    quad_swapped = with_sibling(grad_quad)

    inverse = prepare(ids, diag_blocks)
    grad_blocks = [grad_quad] + grad_far + [quad_swapped] + [with_sibling(b) for b in grad_far]
    solved, own, given, *kept = solve(ids, grad_blocks, inverse, trailing_factor, panel_factor.T)
    trailing_out = trailing_update(ids, [row_even, row_odd], solved, trailing_grad)
    taken = with_neighbour(given)
    taken, trailing_out = lax.optimization_barrier((taken, trailing_out))
    sums = [kept[j] + taken[72 * j : 72 * j + 72] for j in range(4)]
    came = [with_row_partner(sums[j], 2 * j) for j in range(1, 4)]

    total = sums[0] + (came[0] + came[1] + came[2])
    row_out = row_grad - total[0:64, :]
    diag_sum = jnp.concatenate([total[64:72, 0:64], total[64:72, 64:128]], axis=0)
    global_rows = z * 64 + jnp.arange(64)[None, :]
    global_cols = col * 16 + jnp.arange(16)[:, None]
    diag_out = jnp.where(global_rows >= global_cols, diag_grad.T - diag_sum, jnp.float32(0.0))
    return (own.T, trailing_out, row_out, diag_out.T)


def solution(mesh):
    both = P("row", "col")
    return jax.shard_map(
        on_device,
        mesh=mesh,
        in_specs=(both,) * 8,
        out_specs=(both,) * 4,
        check_vma=False,
    )
```
